32 devices in a mesh: dp: 16 (over z, y, core), tensor: 2 (over x).
Axes of the slice: x: 2, y: 2, z: 4, core: 2. Of those that a mesh axis runs over, the one named last changes fastest.
Arguments:
- hidden: bfloat16 [8192, 768], P('dp'), may hold values from -6 to 6
- spatial: bfloat16 [8192, 768], P('dp'), may hold values from -6 to 6
- visual: bfloat16 [8192, 768], P('dp'), may hold values from -6 to 6
- vis_len: int32 [16], P('dp'), may hold values from 256 to 512, as said below
- text_box: int32 [8192], P('dp'), may hold values from 0 to 63
- vis_box: int32 [8192], P('dp'), may hold values from 0 to 63
- text_weight_matrix: bfloat16 [5, 768, 768], P(None, None, 'tensor'), may hold values from -0.21875 to 0.21875
- w_vis: bfloat16 [3, 768, 768], P(None, None, 'tensor'), may hold values from -0.21875 to 0.21875
- w_out: bfloat16 [2, 768, 768], P(None, 'tensor'), may hold values from -0.875 to 0.875
- rel_table: float32 [12, 256], P('tensor'), may hold values from -3 to 3
- space_tables: float32 [2, 12, 128], P(None, 'tensor'), may hold values from -3 to 3
- norm_gain: float32 [2, 768], replicated, may hold values from 0.5 to 1.5
- norm_bias: float32 [2, 768], replicated, may hold values from -2 to 2
- w_up: bfloat16 [768, 3072], P(None, 'tensor'), may hold values from -0.21875 to 0.21875
- b_up: float32 [3072], P('tensor'), may hold values from -2 to 2
- w_down: bfloat16 [3072, 768], P('tensor'), may hold values from -0.109375 to 0.109375
- b_down: float32 [768], replicated, may hold values from -2 to 2
- cotangent: bfloat16 [8192, 768], P('dp'), may hold values from -6 to 6
Outputs:
- result: bfloat16 [8192, 768], P('dp')
- g_hidden: bfloat16 [8192, 768], P('dp')
- g_spatial: float32 [8192, 768], P('dp')
- g_visual: float32 [8192, 768], P('dp')
- g_w_text: float32 [5, 768, 768], P(None, 'dp', 'tensor')
- g_w_vis: float32 [3, 768, 768], P(None, 'dp', 'tensor')
- g_w_out: float32 [2, 768, 768], P(None, 'tensor', 'dp')
- g_rel_table: float32 [12, 256], P('tensor')
- g_space_tables: float32 [2, 12, 128], P(None, 'tensor')
- g_norm_gain: float32 [2, 768], replicated
- g_norm_bias: float32 [2, 768], replicated
- g_w_up: float32 [768, 3072], P('dp', 'tensor')
- g_b_up: float32 [3072], P('tensor')
- g_w_down: float32 [3072, 768], P('tensor', 'dp')
- g_b_down: float32 [768], replicated
The draws below stay inside these ranges and needn't reach their ends.
Inputs may be any that keep to these rules, and one draw needn't show every extreme that they name: `vis_len`: each page has 256 or 512 visual tokens.
All inputs are finite; a program needn't handle non-finite values.
Results may differ from the reference program's by a relative error of at most 0.014.
The reference program's roundings to bfloat16 on the way count: a program that leaves them out, or rounds other values in their place, can miss the bound.
Values sent between devices are 32-bit elements; how exact they have to be, the bound alone decides.
No kernel may reach another device: no remote copies, remote signals or barrier semaphores. Data moves between devices by JAX's collectives and lax.ppermute only.
A program may use at most 320 MiB of HBM per device.

```python
import jax
import jax.numpy as jnp
from jax import lax

D = 768
H = 12
HD = 64
FF = 3072
TEXT = 512
VSLOT = 512
NREL = 256
NBOX = 64
NSPACE = 128
PAGES = 16
TOKENS = 8192
VTOKENS = 8192


def draw_vis_len(key, part):
    key = jax.random.fold_in(key, 3)
    doubled = jax.random.randint(key, (PAGES,), 0, 2)
    doubled = doubled.at[0].set(1).at[1].set(0)
    return (VSLOT // 2 * (1 + doubled)).astype(jnp.int32)


def touch_ends(entries, rng, smallest, top_value):
    spot = [jax.random.randint(jax.random.fold_in(rng, axis), (), 0, length) for axis, length in enumerate(entries.shape)]
    main_axis = entries.shape.index(max(entries.shape))
    beside = spot[:main_axis] + [(spot[main_axis] + 1) % entries.shape[main_axis]] + spot[main_axis + 1:]
    return entries.at[tuple(spot)].set(smallest).at[tuple(beside)].set(top_value)


def levels(own_key, extent, cuts, smallest, largest):
    factor_of = 1.0
    for dim, blocks in cuts:
        steps = jax.random.uniform(jax.random.fold_in(jax.random.fold_in(own_key, 6), dim), (blocks,), jnp.float32, smallest / len(cuts), largest / len(cuts))
        factor_of = factor_of * jnp.repeat(jnp.exp(steps), extent[dim] // blocks).reshape((-1,) + (1,) * (len(extent) - 1 - dim))
    return factor_of


def noise(rng, dims, deviation, bound, split=(), kind=jnp.bfloat16):
    result = jax.random.normal(rng, dims, jnp.float32) * deviation
    if len(split) > 0:
        result = levels(rng, dims, split, -0.22, 0.18) * result
    return jnp.clip(result, min=-bound, max=bound).astype(kind)


def setup_inputs(seed: int = 0) -> dict:
    key_of = jax.random.split(jax.random.key(seed), 19)
    return {
        "hidden": noise(key_of[0], (TOKENS, D), 1.0, 6.0, ((0, 16),)),
        "spatial": noise(key_of[1], (TOKENS, D), 1.0, 6.0, ((0, 16),)),
        "visual": noise(key_of[2], (VTOKENS, D), 1.0, 6.0, ((0, 16),)),
        "vis_len": draw_vis_len(jax.random.fold_in(key_of[18], 71), 0),
        "text_box": touch_ends(jax.random.randint(key_of[4], (TOKENS,), 0, NBOX), jax.random.fold_in(key_of[4], 1), 0, NBOX - 1).astype(jnp.int32),
        "vis_box": touch_ends(jax.random.randint(key_of[5], (VTOKENS,), 0, NBOX), jax.random.fold_in(key_of[5], 1), 0, NBOX - 1).astype(jnp.int32),
        "text_weight_matrix": noise(key_of[6], (5, D, D), D ** -0.5, 0.21875, ((2, 2),)),
        "w_vis": noise(key_of[7], (3, D, D), D ** -0.5, 0.21875, ((2, 2),)),
        "w_out": noise(key_of[8], (2, D, D), (D // 16) ** -0.5, 0.875, ((1, 2),)),
        "rel_table": noise(key_of[9], (H, NREL), 0.5, 3.0, ((0, 2),), jnp.float32),
        "space_tables": noise(key_of[10], (2, H, NSPACE), 0.5, 3.0, ((1, 2),), jnp.float32),
        "norm_gain": jnp.clip(1.0 + 0.1 * jax.random.normal(key_of[11], (2, D), jnp.float32), 0.5, 1.5),
        "norm_bias": noise(key_of[12], (2, D), 0.3, 2.0, (), jnp.float32),
        "w_up": noise(key_of[13], (D, FF), D ** -0.5, 0.21875, ((1, 2),)),
        "b_up": noise(key_of[14], (FF,), 0.3, 2.0, ((0, 2),), jnp.float32),
        "w_down": noise(key_of[15], (FF, D), FF ** -0.5, 0.109375, ((0, 2),)),
        "b_down": noise(key_of[16], (D,), 0.3, 2.0, (), jnp.float32),
        "cotangent": noise(key_of[17], (TOKENS, D), 1.0, 6.0, ((0, 16),)),
    }


@jax.custom_vjp
def low(v):
    return lax.optimization_barrier(v.astype(jnp.bfloat16)).astype(jnp.float32)

@jax.custom_vjp
def low_back(v):
    return v

def low_keep(v):
    return (low(v), None)

def low_pass(kept, grad):
    return (grad,)

def back_keep(v):
    return (v, None)

def back_low(kept, grad):
    return (low(grad),)
low.defvjp(low_keep, low_pass)
low_back.defvjp(back_keep, back_low)

def rounded(values):
    return low_back(low(values))

def matmul_high(left_side, right_side):
    return jnp.dot(left_side, right_side, precision=lax.Precision.HIGHEST)

def einsum_high(pattern, left_side, right_side):
    return jnp.einsum(pattern, left_side, right_side, precision=lax.Precision.HIGHEST)

def layer_norm(values, scales, shifts):
    centred = values - lax.optimization_barrier(jnp.mean(values, -1, keepdims=True))
    variance = lax.optimization_barrier(jnp.mean(centred * centred, -1, keepdims=True))
    return centred * lax.rsqrt(variance + 1e-05) * scales + shifts

def split_heads(values):
    return values.reshape(values.shape[0], -1, HD).transpose(1, 0, 2)

def join_heads(values):
    return values.transpose(1, 0, 2).reshape(values.shape[1], -1)

def forward(weights, hidden, spatial, visual, rel_index, space_index, image_index, valid_keys):
    text_weight_matrix, w_vis, w_out, rel_table, space_tables, norm_gain, norm_bias, w_up, b_up, w_down, b_down = weights
    scale = HD ** (-0.5)
    text_proj = rounded(einsum_high('sd,pde->pse', hidden, text_weight_matrix[:3]))
    space_proj = rounded(einsum_high('sd,pde->pse', spatial, text_weight_matrix[3:]))
    image_query = rounded(matmul_high(hidden, w_vis[0]))
    image_proj = rounded(einsum_high('sd,pde->pse', visual, w_vis[1:]))
    text_query, text_key_rows, text_values = (split_heads(text_proj[0]), split_heads(text_proj[1]), split_heads(text_proj[2]))
    space_query, space_keys = (split_heads(space_proj[0]), split_heads(space_proj[1]))
    image_heads = split_heads(image_query)
    image_keys, image_values = (split_heads(image_proj[0]), split_heads(image_proj[1]))
    text_raw = einsum_high('hqd,hkd->hqk', text_query, text_key_rows) + einsum_high('hqd,hkd->hqk', space_query, space_keys)
    text_scores = low_back(text_raw * scale + jnp.take(rel_table, rel_index, axis=1) + jnp.take(space_tables[0], space_index, axis=1))
    image_raw = einsum_high('hqd,hkd->hqk', image_heads, image_keys) * scale + jnp.take(space_tables[1], image_index, axis=1)
    image_scores = low_back(jnp.where(valid_keys, image_raw, -1e+30))
    text_probs = jax.nn.softmax(text_scores, axis=-1)
    image_probs = jax.nn.softmax(image_scores, axis=-1)
    text_out = rounded(einsum_high('hqk,hkd->hqd', low(text_probs), text_values))
    image_out = rounded(einsum_high('hqk,hkd->hqd', low(image_probs), image_values))
    merged = jnp.concatenate([join_heads(text_out), join_heads(image_out)], 1)
    attention = low_back(matmul_high(merged, w_out.reshape(-1, w_out.shape[2])))
    normed = layer_norm(hidden + attention, norm_gain[0], norm_bias[0])
    pre_gelu = low_back(matmul_high(low(normed), w_up) + b_up)
    activated = low(jax.nn.gelu(pre_gelu, approximate=False))
    feed_out = low_back(matmul_high(activated, w_down) + b_down)
    return layer_norm(normed + feed_out, norm_gain[1], norm_bias[1])

def reference(hidden, spatial, visual, vis_len, text_box, vis_box, text_weight_matrix, w_vis, w_out, rel_table, space_tables, norm_gain, norm_bias, w_up, b_up, w_down, b_down, cotangent):
    weights = tuple((member.astype(jnp.float32) for member in (text_weight_matrix, w_vis, w_out, rel_table, space_tables, norm_gain, norm_bias, w_up, b_up, w_down, b_down)))
    page_count = hidden.shape[0] // TEXT
    width = hidden.shape[1]
    position = jnp.arange(TEXT).astype(jnp.int32)
    rel_index = (jnp.clip(position[None, :] - position[:, None], -(NREL // 2), NREL // 2 - 1) + NREL // 2).astype(jnp.int32)
    slot_index = jnp.arange(VSLOT).astype(jnp.int32)

    def one_page(totals, page_items):
        page_hidden, page_spatial, page_visual, length, page_text_box, page_vis_box, page_cot = page_items
        space_index = (page_text_box[:, None] - page_text_box[None, :] + NBOX).astype(jnp.int32)
        image_index = (page_text_box[:, None] - page_vis_box[None, :] + NBOX).astype(jnp.int32)
        valid_keys = (slot_index < length)[None, None, :]

        def page_forward(layer_weights, hidden_page, spatial_page, visual_page):
            return forward(layer_weights, hidden_page, spatial_page, visual_page, rel_index, space_index, image_index, valid_keys)
        outcome, pull_back = jax.vjp(page_forward, weights, page_hidden.astype(jnp.float32), page_spatial.astype(jnp.float32), page_visual.astype(jnp.float32))
        gradients = pull_back(page_cot.astype(jnp.float32))
        totals = jax.tree.map(jnp.add, totals, gradients[0])
        return (totals, (outcome.astype(jnp.bfloat16), gradients[1].astype(jnp.bfloat16), gradients[2], gradients[3]))
    zero_totals = jax.tree.map(jnp.zeros_like, weights)
    page_inputs = (hidden.reshape(page_count, TEXT, width), spatial.reshape(page_count, TEXT, width), visual.reshape(page_count, VSLOT, width), vis_len, text_box.reshape(page_count, TEXT), vis_box.reshape(page_count, VSLOT), cotangent.reshape(page_count, TEXT, width))
    totals, page_results = lax.scan(one_page, zero_totals, page_inputs)
    return (page_results[0].reshape(-1, width), page_results[1].reshape(-1, width), page_results[2].reshape(-1, width), page_results[3].reshape(-1, width), totals[0], totals[1], totals[2], totals[3], totals[4], totals[5], totals[6], totals[7], totals[8], totals[9], totals[10])
```

```python
from functools import partial

import jax
import jax.numpy as jnp
from jax import lax
from jax.experimental import pallas as pl
from jax.experimental.pallas import tpu as pltpu
from jax.sharding import PartitionSpec as P

HD = 64
PAIR = 2 * HD
TEXT = 512
NREL = 256
NBOX = 64
BLK = 128
EPSILON = 1e-05
MASKED = -1e30
SCALE = HD ** (-0.5)
F32 = jnp.float32
BF16 = jnp.bfloat16
MIB = 1 << 20


def mm(a, b):
    return jnp.dot(a, b, preferred_element_type=F32)


def mm_nt(a, b):
    return lax.dot_general(a, b, (((1,), (1,)), ((), ())), preferred_element_type=F32)


def mm_tn(a, b):
    return lax.dot_general(a, b, (((0,), (0,)), ((), ())), preferred_element_type=F32)


def call(body, name, grid, args, in_specs, outs, out_specs, scratch=(), flops=0, nbytes=0):
    return pl.pallas_call(
        body,
        out_shape=outs,
        grid_spec=pltpu.PrefetchScalarGridSpec(
            num_scalar_prefetch=0,
            grid=grid,
            in_specs=in_specs,
            out_specs=out_specs,
            scratch_shapes=list(scratch),
        ),
        compiler_params=pltpu.CompilerParams(
            dimension_semantics=("arbitrary",) * len(grid), vmem_limit_bytes=44 * MIB
        ),
        cost_estimate=pl.CostEstimate(flops=int(flops), bytes_accessed=int(nbytes), transcendentals=0),
        name=name,
    )(*args)


def whole(x):
    nd = x.ndim
    return pl.BlockSpec(x.shape, lambda p: (0,) * nd)


def sds(shape, dtype=F32):
    return jax.ShapeDtypeStruct(shape, dtype)


def pair_block(rows, width):
    return pl.BlockSpec((rows, width), lambda p: (0, p))


def lead_block(x):
    nd = x.ndim
    return pl.BlockSpec((1,) + x.shape[1:], lambda p: (p,) + (0,) * (nd - 1))


def proj_body(hid, spa, vis, wt, wv, tqs, tks, tv, vq, vk, vv):
    ph = mm(hid[...], jnp.concatenate([wt[0], wt[1], wt[2], wv[0]], 1)).astype(BF16)
    ps = mm(spa[...], jnp.concatenate([wt[3], wt[4]], 1)).astype(BF16)
    pv = mm(vis[...], jnp.concatenate([wv[1], wv[2]], 1)).astype(BF16)
    scale = jnp.asarray(SCALE, BF16)
    tqs[0, :, :PAIR] = ph[:, :PAIR] * scale
    tqs[0, :, PAIR:] = ps[:, :PAIR] * scale
    tks[0, :, :PAIR] = ph[:, PAIR : 2 * PAIR]
    tks[0, :, PAIR:] = ps[:, PAIR:]
    tv[0] = ph[:, 2 * PAIR : 3 * PAIR]
    vq[0] = ph[:, 3 * PAIR :] * scale
    vk[0] = pv[:, :PAIR]
    vv[0] = pv[:, PAIR:]


def projections(hidden, spatial, visual, w_text, w_vis):
    n, d = hidden.shape
    pairs = w_text.shape[2] // PAIR
    wide, slim = sds((pairs, n, 2 * PAIR), BF16), sds((pairs, n, PAIR), BF16)
    outs = [wide, wide, slim, slim, slim, slim]
    return call(
        proj_body,
        "projections",
        (pairs,),
        (hidden, spatial, visual, w_text, w_vis),
        [
            whole(hidden),
            whole(spatial),
            whole(visual),
            pl.BlockSpec((5, d, PAIR), lambda p: (0, 0, p)),
            pl.BlockSpec((3, d, PAIR), lambda p: (0, 0, p)),
        ],
        outs,
        [lead_block(o) for o in outs],
        flops=2 * n * d * 8 * pairs * PAIR,
        nbytes=9e6,
    )


def head_mask(h, width):
    lane = lax.broadcasted_iota(jnp.int32, (1, width), 1)
    return jnp.where((lane // HD) % 2 == h, 1.0, 0.0).astype(BF16)


def one_hot(box):
    lane = lax.broadcasted_iota(jnp.int32, (box.shape[0], PAIR), 1)
    return jnp.where(lane % HD == box, 1.0, 0.0).astype(BF16)


def box_rows(reversed_row):
    wide = jnp.broadcast_to(reversed_row, (NBOX, PAIR))
    rolled = pltpu.roll(wide, NBOX + 1, 1, stride=1, stride_axis=0)
    high = rolled.astype(BF16).astype(F32)
    rest = pltpu.roll(rolled - high, NBOX, 1)
    lane = lax.broadcasted_iota(jnp.int32, (NBOX, PAIR), 1)
    both = jnp.where(lane < NBOX, high, rest)
    return jnp.concatenate([both, jnp.zeros_like(both)], 0).astype(BF16)


def rel_band(extended_row):
    wide = jnp.broadcast_to(extended_row, (BLK, 4 * BLK))
    return pltpu.roll(wide, 0, 1, stride=1, stride_axis=0)[:, BLK:]


def rel_bias(band, ends, block, blocks):
    pieces = []
    for other in range(blocks):
        step = other - block
        if step >= 2:
            pieces.append(jnp.broadcast_to(ends[1], (BLK, BLK)))
        elif step <= -2:
            pieces.append(jnp.broadcast_to(ends[0], (BLK, BLK)))
        else:
            pieces.append(band[:, (step + 1) * BLK : (step + 2) * BLK])
    return jnp.concatenate(pieces, 1)


def rel_parts(rel, h):
    row = rel[0, h : h + 1, :]
    return rel_band(row), (row[:, :1], row[:, 4 * BLK - 1 :])


def attend(scores, values):
    peak = jnp.max(scores, 1, keepdims=True)
    powers = jnp.exp(scores - peak)
    total = jnp.sum(powers, 1, keepdims=True)
    probs = (powers * (1.0 / total)).astype(BF16)
    return mm(probs, values), peak + jnp.log(total)


def forward_body(vlen, tqs, vq, tks, tv, vk, vv, tbq, tbk, vbk, rel, rows, wo, attn, to, vo, lse, *, first):
    count = tqs.shape[1]
    keys_n = tks.shape[1]
    hot_q, hot_t, hot_v = one_hot(tbq[...]), one_hot(tbk[...]), one_hot(vbk[...])
    keys_t = jnp.concatenate([tks[0], hot_t], 1)
    keys_v = jnp.concatenate([vk[0], hot_v], 1)
    valid = lax.broadcasted_iota(jnp.int32, (1, keys_n), 1) < vlen[0]
    lane = lax.broadcasted_iota(jnp.int32, (BLK, PAIR), 1)
    text_out, vis_out, logs = {}, {}, {}
    for h in range(2):
        look_t = mm(hot_q, box_rows(rows[0, 0, h : h + 1, :])).astype(BF16)
        look_v = mm(hot_q, box_rows(rows[0, 1, h : h + 1, :])).astype(BF16)
        query_t = jnp.concatenate([tqs[0] * head_mask(h, 2 * PAIR), look_t], 1)
        query_v = jnp.concatenate([vq[0] * head_mask(h, PAIR), look_v], 1)
        band, ends = rel_parts(rel, h)
        for b in range(count // BLK):
            part = slice(b * BLK, (b + 1) * BLK)
            bias = rel_bias(band, ends, first // BLK + b, keys_n // BLK)
            text_out[h, b], logs[0, h, b] = attend(mm_nt(query_t[part], keys_t) + bias, tv[0])
            vis_out[h, b], logs[1, h, b] = attend(
                jnp.where(valid, mm_nt(query_v[part], keys_v), MASKED), vv[0]
            )
    weights = jnp.concatenate([wo[0], wo[1]], 0)
    for b in range(count // BLK):
        part = slice(b * BLK, (b + 1) * BLK)
        out_t = jnp.where(lane < HD, text_out[0, b], text_out[1, b]).astype(BF16)
        out_v = jnp.where(lane < HD, vis_out[0, b], vis_out[1, b]).astype(BF16)
        to[part, :] = out_t
        vo[part, :] = out_v
        kept = jnp.zeros((BLK, PAIR), F32)
        for spot, (stream, h) in enumerate(((0, 0), (0, 1), (1, 0), (1, 1))):
            kept = jnp.where(lane == spot, logs[stream, h, b], kept)
        lse[0, part, :] = kept
        term = mm(jnp.concatenate([out_t, out_v], 1), weights)

        @pl.when(pl.program_id(0) == 0)
        def _():
            attn[part, :] = term

        @pl.when(pl.program_id(0) > 0)
        def _():
            attn[part, :] += term


def forward_rows(first, count, proj, boxes, vlen, rel_ext, box_rev, w_out):
    tqs, tks, tv, vq, vk, vv = proj
    tb, vb = boxes
    pairs, n, _ = tqs.shape
    d = w_out.shape[2]
    spot = first // count

    def rows_of(x):
        return pl.BlockSpec((1, count, x.shape[2]), lambda p: (p, spot, 0))

    return call(
        partial(forward_body, first=first),
        f"attention_forward_{spot}",
        (pairs,),
        (vlen, tqs, vq, tks, tv, vk, vv, tb, tb, vb, rel_ext, box_rev, w_out),
        [
            pl.BlockSpec(memory_space=pltpu.SMEM),
            rows_of(tqs),
            rows_of(vq),
            lead_block(tks),
            lead_block(tv),
            lead_block(vk),
            lead_block(vv),
            pl.BlockSpec((count, 1), lambda p: (spot, 0)),
            whole(tb),
            whole(vb),
            lead_block(rel_ext),
            lead_block(box_rev),
            pl.BlockSpec((2, PAIR, d), lambda p: (0, p, 0)),
        ],
        [
            sds((count, d)),
            sds((count, pairs * PAIR), BF16),
            sds((count, pairs * PAIR), BF16),
            sds((pairs, count, PAIR)),
        ],
        [
            pl.BlockSpec((count, d), lambda p: (0, 0)),
            pair_block(count, PAIR),
            pair_block(count, PAIR),
            pl.BlockSpec((1, count, PAIR), lambda p: (p, 0, 0)),
        ],
        flops=pairs * 2 * 10 * count * n * PAIR,
        nbytes=4e6,
    )


def scores_gradient(probs, grad_out, values):
    grad_probs = mm_nt(grad_out, values)
    inner = jnp.sum(grad_probs * probs, 1, keepdims=True)
    return (probs * (grad_probs - inner)).astype(BF16)


def box_gradient(hot_q, spread, out):
    lane = lax.broadcasted_iota(jnp.int32, (hot_q.shape[0], NBOX), 1)
    flipped = jnp.where(lane == NBOX - 1 - hot_q, 1.0, 0.0).astype(BF16)
    high = spread.astype(BF16)
    rest = (spread - high.astype(F32)).astype(BF16)
    table = mm_tn(flipped, high) + mm_tn(flipped, rest)
    lane = lax.broadcasted_iota(jnp.int32, (NBOX, PAIR), 1)
    for h in range(2):
        mine = table if h == 0 else pltpu.roll(table, NBOX, 1)
        mine = jnp.where(lane < NBOX, mine, 0.0)
        sheared = pltpu.roll(mine, 0, 1, stride=1, stride_axis=0)
        out[0, h : h + 1, :] = jnp.sum(sheared, 0, keepdims=True)


def shear_sum(band):
    width = band.shape[1]
    rows = BLK
    while rows > 8:
        rows //= 2
        band = band[:rows] + pltpu.roll(band[rows:], width - rows, 1)
    row = lax.broadcasted_iota(jnp.int32, band.shape, 0)
    for bit in (4, 2, 1):
        band = jnp.where((row // bit) % 2 == 1, pltpu.roll(band, width - bit, 1), band)
    return jnp.sum(band, 0, keepdims=True)


def visual_back_body(
    vlen, vq, vk, vv, dvo, lse, tb, vb, rows, wv, dxq, dxv, g_vis, g_box, ds_ref, pb_ref
):
    n = vq.shape[1]
    hot_q, hot_v = one_hot(tb[...]), one_hot(vb[...])
    keys = jnp.concatenate([vk[0], hot_v], 1)
    valid = lax.broadcasted_iota(jnp.int32, (1, vk.shape[1]), 1) < vlen[0]
    dq = dkt = dvt = spread = None
    for h in range(2):
        mask = head_mask(h, PAIR)
        look = mm(hot_q, box_rows(rows[0, 1, h : h + 1, :])).astype(BF16)
        mine = vq[0] * mask
        query = jnp.concatenate([mine, look], 1)
        grad = dvo[...] * mask
        for b in range(n // BLK):
            part = slice(b * BLK, (b + 1) * BLK)
            scores = jnp.where(valid, mm_nt(query[part], keys), MASKED)
            probs = jnp.exp(scores - lse[0, part, 2 + h : 3 + h])
            pb_ref[part, :] = probs.astype(BF16)
            ds_ref[part, :] = scores_gradient(probs, grad[part], vv[0])
        ds, pb = ds_ref[...], pb_ref[...]
        terms = (mm(ds, vk[0] * mask), mm_tn(mine, ds), mm_tn(grad, pb), mm(ds, hot_v * mask))
        if h == 0:
            dq, dkt, dvt, spread = terms
        else:
            dq, dkt, dvt, spread = (a + b for a, b in zip((dq, dkt, dvt, spread), terms))
    box_gradient(tb[...], spread, g_box)
    dxq[...] = (dq * SCALE).astype(BF16)
    both = jnp.concatenate([dkt.astype(BF16), dvt.astype(BF16)], 0).T
    dxv[...] = both
    term = mm_nt(both, jnp.concatenate([wv[1], wv[2]], 1))

    @pl.when(pl.program_id(0) == 0)
    def _():
        g_vis[...] = term

    @pl.when(pl.program_id(0) > 0)
    def _():
        g_vis[...] += term


def visual_back(proj, boxes, vlen, box_rev, dvo, lse, w_vis):
    vq, vk, vv = proj[3:]
    tb, vb = boxes
    pairs, n, _ = vq.shape
    d = w_vis.shape[1]
    return call(
        visual_back_body,
        "visual_attention_backward",
        (pairs,),
        (vlen, vq, vk, vv, dvo, lse, tb, vb, box_rev, w_vis),
        [
            pl.BlockSpec(memory_space=pltpu.SMEM),
            lead_block(vq),
            lead_block(vk),
            lead_block(vv),
            pair_block(n, PAIR),
            lead_block(lse),
            whole(tb),
            whole(vb),
            lead_block(box_rev),
            pl.BlockSpec((3, d, PAIR), lambda p: (0, 0, p)),
        ],
        [
            sds((n, pairs * PAIR), BF16),
            sds((n, pairs * 2 * PAIR), BF16),
            sds((n, d)),
            sds((pairs, 8, PAIR)),
        ],
        [
            pair_block(n, PAIR),
            pair_block(n, 2 * PAIR),
            pl.BlockSpec((n, d), lambda p: (0, 0)),
            pl.BlockSpec((1, 8, PAIR), lambda p: (p, 0, 0)),
        ],
        [pltpu.VMEM((n, n), BF16), pltpu.VMEM((n, n), BF16)],
        flops=pairs * 2 * 18 * n * n * PAIR,
        nbytes=5e6,
    )


def text_back_body(
    tqs, tks, tv, dto, lse, tb, rel, rows, dxq, wt, wv, dxh, dxs, g_hid, g_spa, g_box, g_rel, ds_ref, pb_ref
):
    n = tqs.shape[1]
    hot = one_hot(tb[...])
    keys = jnp.concatenate([tks[0], hot], 1)
    dq = dkt = dvt = spread = None
    for h in range(2):
        mask, wide_mask = head_mask(h, PAIR), head_mask(h, 2 * PAIR)
        look = mm(hot, box_rows(rows[0, 0, h : h + 1, :])).astype(BF16)
        mine = tqs[0] * wide_mask
        query = jnp.concatenate([mine, look], 1)
        grad = dto[...] * mask
        band, ends = rel_parts(rel, h)
        near = [None] * 3
        low = high = jnp.zeros((BLK, BLK), F32)
        for b in range(n // BLK):
            part = slice(b * BLK, (b + 1) * BLK)
            scores = mm_nt(query[part], keys) + rel_bias(band, ends, b, n // BLK)
            probs = jnp.exp(scores - lse[0, part, h : h + 1])
            pb_ref[part, :] = probs.astype(BF16)
            ds = scores_gradient(probs, grad[part], tv[0])
            ds_ref[part, :] = ds
            ds = ds.astype(F32)
            for other in range(n // BLK):
                piece = ds[:, other * BLK : (other + 1) * BLK]
                step = other - b
                if step >= 2:
                    high = high + piece
                elif step <= -2:
                    low = low + piece
                else:
                    near[step + 1] = piece if near[step + 1] is None else near[step + 1] + piece
        ds, pb = ds_ref[...], pb_ref[...]
        sums = shear_sum(jnp.concatenate(near + [jnp.zeros((BLK, BLK), F32)], 1))
        far = jnp.concatenate(
            [jnp.sum(low, 0, keepdims=True), jnp.sum(high, 0, keepdims=True)], 1
        )
        g_rel[0, 2 * h : 2 * h + 1, :] = sums
        g_rel[0, 2 * h + 1 : 2 * h + 2, : 2 * BLK] = far
        terms = (mm(ds, tks[0] * wide_mask), mm_tn(mine, ds), mm_tn(grad, pb), mm(ds, hot * mask))
        if h == 0:
            dq, dkt, dvt, spread = terms
        else:
            dq, dkt, dvt, spread = (a + b for a, b in zip((dq, dkt, dvt, spread), terms))
    box_gradient(tb[...], spread, g_box)
    dqs = (dq * SCALE).astype(BF16)
    rest = jnp.concatenate([dkt.astype(BF16), dvt.astype(BF16)], 0).T
    to_spatial = jnp.concatenate([dqs[:, PAIR:], rest[:, PAIR : 2 * PAIR]], 1)
    to_hidden = jnp.concatenate([dqs[:, :PAIR], rest[:, :PAIR], rest[:, 2 * PAIR :]], 1)
    dxs[...] = to_spatial
    dxh[...] = to_hidden
    term_s = mm_nt(to_spatial, jnp.concatenate([wt[3], wt[4]], 1))
    term_h = mm_nt(
        jnp.concatenate([to_hidden, dxq[...]], 1),
        jnp.concatenate([wt[0], wt[1], wt[2], wv[0]], 1),
    )

    @pl.when(pl.program_id(0) == 0)
    def _():
        g_spa[...] = term_s
        g_hid[...] = term_h

    @pl.when(pl.program_id(0) > 0)
    def _():
        g_spa[...] += term_s
        g_hid[...] += term_h


def text_back(proj, boxes, rel_ext, box_rev, dto, lse, dxq, w_text, w_vis):
    tqs, tks, tv = proj[:3]
    tb = boxes[0]
    pairs, n, _ = tqs.shape
    d = w_vis.shape[1]
    return call(
        text_back_body,
        "text_attention_backward",
        (pairs,),
        (tqs, tks, tv, dto, lse, tb, rel_ext, box_rev, dxq, w_text, w_vis),
        [
            lead_block(tqs),
            lead_block(tks),
            lead_block(tv),
            pair_block(n, PAIR),
            lead_block(lse),
            whole(tb),
            lead_block(rel_ext),
            lead_block(box_rev),
            pair_block(n, PAIR),
            pl.BlockSpec((5, d, PAIR), lambda p: (0, 0, p)),
            pl.BlockSpec((3, d, PAIR), lambda p: (0, 0, p)),
        ],
        [
            sds((n, pairs * 3 * PAIR), BF16),
            sds((n, pairs * 2 * PAIR), BF16),
            sds((n, d)),
            sds((n, d)),
            sds((pairs, 8, PAIR)),
            sds((pairs, 8, 4 * BLK)),
        ],
        [
            pair_block(n, 3 * PAIR),
            pair_block(n, 2 * PAIR),
            pl.BlockSpec((n, d), lambda p: (0, 0)),
            pl.BlockSpec((n, d), lambda p: (0, 0)),
            pl.BlockSpec((1, 8, PAIR), lambda p: (p, 0, 0)),
            pl.BlockSpec((1, 8, 4 * BLK), lambda p: (p, 0, 0)),
        ],
        [pltpu.VMEM((n, n), BF16), pltpu.VMEM((n, n), BF16)],
        flops=pairs * 2 * 26 * n * n * PAIR,
        nbytes=9e6,
    )


def normalise(values):
    centred = values - jnp.mean(values, 1, keepdims=True)
    rstd = lax.rsqrt(jnp.mean(centred * centred, 1, keepdims=True) + EPSILON)
    return centred * rstd, rstd


def norm_back(grad, unit, rstd, gain):
    scaled = grad * gain
    mean_one = jnp.mean(scaled, 1, keepdims=True)
    mean_two = jnp.mean(scaled * unit, 1, keepdims=True)
    return rstd * (scaled - mean_one - unit * mean_two)


def column_sum(x):
    return jnp.sum(x, 0, keepdims=True)


def up_body(hid, own, got, norms, w_up, b_up, w_down, r1, h1, h1b, z, slope, f):
    total = hid[...].astype(F32) + (own[...] + got[...])
    unit, _ = normalise(total)
    normed = unit * norms[0:1, :] + norms[2:3, :]
    low = normed.astype(BF16)
    r1[...] = total
    h1[...] = normed
    h1b[...] = low
    u = mm(low, w_up[...]) + b_up[...]
    cdf = 0.5 * (1.0 + lax.erf(u * (0.5**0.5)))
    slope[...] = cdf + u * (jnp.exp(-0.5 * u * u) * 0.3989422804014327)
    active = (u * cdf).astype(BF16)
    z[...] = active
    f[...] = mm(active, w_down[...])


def up_rows(spot, hidden, own, got, norms, w_up, b_up, w_down):
    count, d = own.shape
    ff = w_up.shape[1]
    args = (hidden, own, got, norms, w_up, b_up, w_down)
    outs = [sds((count, d)), sds((count, d)), sds((count, d), BF16), sds((count, ff), BF16)]
    outs += [sds((count, ff)), sds((count, d))]
    return call(
        up_body,
        f"feed_forward_{spot}",
        (1,),
        args,
        [pl.BlockSpec((count, d), lambda p: (spot, 0))] + [whole(x) for x in args[1:]],
        outs,
        [whole(x) for x in outs],
        flops=4 * count * d * ff,
        nbytes=9e6,
    )


def down_body(h1, own, got, cot, norms, b_down, w_down, w_up, slope, result, dr2, df, du, pd, sums, sum_up):
    total = h1[...] + ((own[...] + got[...]) + b_down[...])
    unit, rstd = normalise(total)
    result[...] = (unit * norms[1:2, :] + norms[3:4, :]).astype(BF16)
    grad = cot[...].astype(F32)
    back = norm_back(grad, unit, rstd, norms[1:2, :])
    low = back.astype(BF16)
    dr2[...] = back
    df[...] = low
    grad_u = (slope[...] * mm_nt(low, w_down[...])).astype(BF16)
    du[...] = grad_u
    pd[...] = mm_nt(grad_u, w_up[...])
    sums[0:1, :] = column_sum(grad * unit)
    sums[1:2, :] = column_sum(grad)
    sums[2:3, :] = column_sum(low.astype(F32))
    sum_up[0:1, :] = column_sum(grad_u.astype(F32))


def down_rows(spot, h1, own, got, cotangent, norms, b_down, w_down, w_up, slope):
    count, d = own.shape
    ff = w_up.shape[1]
    args = (h1, own, got, cotangent, norms, b_down, w_down, w_up, slope)
    specs = [whole(x) for x in args]
    specs[3] = pl.BlockSpec((count, d), lambda p: (spot, 0))
    outs = [sds((count, d), BF16), sds((count, d)), sds((count, d), BF16), sds((count, ff), BF16)]
    outs += [sds((count, d)), sds((8, d)), sds((8, ff))]
    return call(
        down_body,
        f"feed_forward_backward_{spot}",
        (1,),
        args,
        specs,
        outs,
        [whole(x) for x in outs],
        flops=4 * count * d * ff,
        nbytes=9e6,
    )


def first_body(dr2, own, got, r1, norms, w_out, dr1, da, dto, dvo, sums):
    grad = dr2[...] + (own[...] + got[...])
    unit, rstd = normalise(r1[...])
    back = norm_back(grad, unit, rstd, norms[0:1, :])
    low = back.astype(BF16)
    dr1[...] = back
    da[...] = low
    dto[...] = mm_nt(low, w_out[0]).astype(BF16)
    dvo[...] = mm_nt(low, w_out[1]).astype(BF16)
    sums[0:1, :] = column_sum(grad * unit)
    sums[1:2, :] = column_sum(grad)


def first_rows(spot, dr2, own, got, r1, norms, w_out):
    count, d = own.shape
    width = w_out.shape[1]
    args = (dr2, own, got, r1, norms, w_out)
    outs = [sds((count, d)), sds((count, d), BF16)]
    outs += [sds((count, width), BF16), sds((count, width), BF16), sds((8, d))]
    return call(
        first_body,
        f"first_norm_backward_{spot}",
        (1,),
        args,
        [whole(x) for x in args],
        outs,
        [whole(x) for x in outs],
        flops=4 * count * d * width,
        nbytes=4e6,
    )


def product_body(a, b, mine, other):
    half = mine.shape[0]
    out = mm(a[...], b[...])
    mine[...] = out[:half]
    other[...] = out[half:]


def weight_product(name, rows_t, cols, block):
    d, n = rows_t.shape
    width = cols.shape[1]
    return call(
        product_body,
        name,
        (width // block,),
        (rows_t, cols),
        [whole(rows_t), pair_block(n, block)],
        [sds((d // 2, width)), sds((d // 2, width))],
        [pair_block(d // 2, block), pair_block(d // 2, block)],
        flops=2 * d * n * width,
        nbytes=4 * d * width,
    )


def attention_product_body(hid, spa, dxh, dxq, dxs, mine, other):
    half = mine.shape[0]
    out = mm(hid[...], jnp.concatenate([dxh[...], dxq[...]], 1))
    cut = out.shape[1]
    mine[:, :cut] = out[:half]
    other[:, :cut] = out[half:]
    out = mm(spa[...], dxs[...])
    mine[:, cut:] = out[:half]
    other[:, cut:] = out[half:]


def attention_product(hid_t, spa_t, dxh, dxq, dxs):
    d, n = hid_t.shape
    pairs = dxq.shape[1] // PAIR
    width = 6 * PAIR
    return call(
        attention_product_body,
        "text_projection_gradients",
        (pairs,),
        (hid_t, spa_t, dxh, dxq, dxs),
        [
            whole(hid_t),
            whole(spa_t),
            pair_block(n, 3 * PAIR),
            pair_block(n, PAIR),
            pair_block(n, 2 * PAIR),
        ],
        [sds((d // 2, pairs * width)), sds((d // 2, pairs * width))],
        [pair_block(d // 2, width), pair_block(d // 2, width)],
        flops=2 * d * n * width * pairs,
        nbytes=4 * d * width * pairs,
    )


class Links:
    def __init__(self, sizes):
        self.n = sizes["dp"]
        self.tensor = sizes["tensor"]
        n = self.n
        self.core = [(d, d ^ 1) for d in range(n)]
        self.side = [(d, d ^ 2) for d in range(n)]
        self.ring = [(d, (d + 4) % n) for d in range(n)]
        self.turns = n // 4

    def order(self):
        me = lax.axis_index("dp")
        core, side, ring = me % 2, (me // 2) % 2, me // 4
        places = []
        for c in range(2):
            for s in range(2):
                for r in range(self.turns):
                    places.append(((ring + r) % self.turns) * 4 + (side ^ s) * 2 + (core ^ c))
        return jnp.stack(places)

    def relative_rows(self, x):
        d = x.shape[1]
        rows = d // self.n
        chunks = x.T.reshape(self.n, rows, x.shape[0])
        return jnp.take(chunks, self.order(), axis=0, mode="clip").reshape(d, x.shape[0])

    def across(self, x):
        return lax.ppermute(x, "tensor", [(0, 1), (1, 0)])

    def scatter(self, halves, side_first):
        mine, other = halves
        width = mine.shape[1]
        rows = mine.shape[0] // (2 * self.turns)
        shape = (2, self.turns, rows, width)
        total = mine.reshape(shape) + lax.ppermute(other, "dp", self.core).reshape(shape)
        if side_first:
            total = total[0] + lax.ppermute(total[1], "dp", self.side)
            moving = total[self.turns - 1]
            for turn in range(self.turns - 2, -1, -1):
                moving = total[turn] + lax.ppermute(moving, "dp", self.ring)
            return moving
        moving = total[:, self.turns - 1]
        for turn in range(self.turns - 2, -1, -1):
            moving = total[:, turn] + lax.ppermute(moving, "dp", self.ring)
        return moving[0] + lax.ppermute(moving[1], "dp", self.side)

    def sum_all(self, x):
        step = 1
        while step < self.n:
            x = x + lax.ppermute(x, "dp", [(d, d ^ step) for d in range(self.n)])
            step *= 2
        return x


def on_device(
    links,
    hidden,
    spatial,
    visual,
    vis_len,
    text_box,
    vis_box,
    text_weight_matrix,
    w_vis,
    w_out,
    rel_table,
    space_tables,
    norm_gain,
    norm_bias,
    w_up,
    b_up,
    w_down,
    b_down,
    cotangent,
):
    n, d = hidden.shape
    width = w_vis.shape[2]
    pairs = width // PAIR
    ff = w_up.shape[1]
    heads = rel_table.shape[0]
    boxes = (text_box.reshape(n, 1), vis_box.reshape(-1, 1))
    rel_ext = jnp.concatenate(
        [
            jnp.broadcast_to(rel_table[:, :1], (heads, NREL // 2)),
            rel_table,
            jnp.broadcast_to(rel_table[:, NREL - 1 :], (heads, NREL // 2)),
        ],
        1,
    ).reshape(pairs, 2, 2 * NREL)
    box_rev = space_tables[:, :, ::-1].reshape(2, pairs, 2, PAIR).transpose(1, 0, 2, 3)
    norms = jnp.concatenate([norm_gain, norm_bias], 0)
    b_up_row, b_down_row = b_up.reshape(1, ff), b_down.reshape(1, d)

    proj = projections(hidden, spatial, visual, text_weight_matrix, w_vis)
    count = n // 2
    spots = range(n // count)
    front = [
        forward_rows(s * count, count, proj, boxes, vis_len, rel_ext, box_rev, w_out) for s in spots
    ]
    got = [links.across(f[0]) for f in front]
    up = [
        up_rows(s, hidden, front[s][0], got[s], norms, w_up, b_up_row, w_down) for s in spots
    ]
    got = [links.across(u[5]) for u in up]
    down = [
        down_rows(s, up[s][1], up[s][5], got[s], cotangent, norms, b_down_row, w_down, w_up, up[s][4])
        for s in spots
    ]
    got = [links.across(x[4]) for x in down]
    first = [first_rows(s, down[s][1], down[s][4], got[s], up[s][0], norms, w_out) for s in spots]

    def joined(parts, axis=0):
        return jnp.concatenate(list(parts), axis)

    result = joined(x[0] for x in down)
    dr1 = joined(x[0] for x in first)
    dto = joined(x[2] for x in first)
    dvo = joined(x[3] for x in first)
    lse = joined((f[3] for f in front), 1)

    dxq, dxv, part_vis, g_box_vis = visual_back(proj, boxes, vis_len, box_rev, dvo, lse, w_vis)
    dxh, dxs, part_hid, part_spa, g_box_text, g_rel = text_back(
        proj, boxes, rel_ext, box_rev, dto, lse, dxq, text_weight_matrix, w_vis
    )
    grad_visual = part_vis + links.across(part_vis)
    grad_spatial = part_spa + links.across(part_spa)
    grad_hidden = (dr1 + (part_hid + links.across(part_hid))).astype(BF16)

    df_t = links.relative_rows(joined(x[2] for x in down))
    h1_t = links.relative_rows(joined(u[2] for u in up))
    da_t = links.relative_rows(joined(x[1] for x in first))
    vis_t = links.relative_rows(visual)
    hid_t = links.relative_rows(hidden)
    spa_t = links.relative_rows(spatial)
    merged = jnp.concatenate([joined(f[1] for f in front), joined(f[2] for f in front)], 1)
    half_down = weight_product("down_gradient", df_t, joined(u[3] for u in up), ff // 2)
    half_up = weight_product("up_gradient", h1_t, joined(x[3] for x in down), ff // 2)
    half_out = weight_product("out_gradient", da_t, merged, width)
    half_vis = weight_product("visual_projection_gradients", vis_t, dxv, width)
    half_text = attention_product(hid_t, spa_t, dxh, dxq, dxs)

    g_w_down = links.scatter(half_down, True).T
    g_w_up = links.scatter(half_up, True)
    rows = d // links.n
    g_w_out = links.scatter(half_out, False).reshape(rows, 2, width).transpose(1, 2, 0)
    from_vis = links.scatter(half_vis, False).reshape(rows, pairs, 2, PAIR)
    from_text = links.scatter(half_text, True).reshape(rows, pairs, 6, PAIR)
    from_vis = from_vis.transpose(2, 0, 1, 3).reshape(2, rows, width)
    from_text = from_text.transpose(2, 0, 1, 3).reshape(6, rows, width)
    g_w_text = jnp.concatenate([from_text[:3], from_text[4:]], 0)
    g_w_vis = jnp.concatenate([from_text[3:4], from_vis], 0)

    rel = g_rel.reshape(pairs, 4, 2, 2 * NREL)[:, :2].reshape(heads, 2, 2 * NREL)
    near, far = rel[:, 0], rel[:, 1]
    half = NREL // 2
    low = jnp.sum(near[:, 3 * half + 1 :], 1) + near[:, 0] + jnp.sum(far[:, :half], 1)
    high = jnp.sum(near[:, 2 * half - 1 : 3 * half], 1) + jnp.sum(far[:, half : 2 * half], 1)
    g_rel_table = jnp.concatenate([low[:, None], near[:, 1 : 2 * half - 1], high[:, None]], 1)
    g_space = jnp.stack([g_box_text[:, :2], g_box_vis[:, :2]]).reshape(2, heads, PAIR)[:, :, ::-1]
    sums_two = sum(x[5] for x in down)
    sums_up = sum(x[6] for x in down)
    sums_one = sum(x[4] for x in first)
    small = jnp.concatenate(
        [
            g_rel_table.reshape(-1),
            g_space.reshape(-1),
            sums_one[0],
            sums_two[0],
            sums_one[1],
            sums_two[1],
            sums_up[0],
            sums_two[2],
        ]
    ).reshape(-1, PAIR)
    small = links.sum_all(small).reshape(-1)
    cuts, at = [], 0
    for shape in ((heads, NREL), (2, heads, PAIR), (2, d), (2, d), (ff,), (d,)):
        size = 1
        for s in shape:
            size *= s
        cuts.append(small[at : at + size].reshape(shape))
        at += size
    return (
        result,
        grad_hidden,
        grad_spatial,
        grad_visual,
        g_w_text,
        g_w_vis,
        g_w_out,
        cuts[0],
        cuts[1],
        cuts[2],
        cuts[3],
        g_w_up,
        cuts[4],
        g_w_down,
        cuts[5],
    )


def solution(mesh):
    return jax.shard_map(
        partial(on_device, Links(dict(mesh.shape))),
        mesh=mesh,
        in_specs=(
            P("dp", None),
            P("dp", None),
            P("dp", None),
            P("dp"),
            P("dp"),
            P("dp"),
            P(None, None, "tensor"),
            P(None, None, "tensor"),
            P(None, "tensor", None),
            P("tensor", None),
            P(None, "tensor", None),
            P(),
            P(),
            P(None, "tensor"),
            P("tensor"),
            P("tensor", None),
            P(),
            P("dp", None),
        ),
        out_specs=(
            P("dp", None),
            P("dp", None),
            P("dp", None),
            P("dp", None),
            P(None, "dp", "tensor"),
            P(None, "dp", "tensor"),
            P(None, "tensor", "dp"),
            P("tensor", None),
            P(None, "tensor", None),
            P(),
            P(),
            P("dp", "tensor"),
            P("tensor"),
            P("tensor", "dp"),
            P(),
        ),
        check_vma=False,
    )
```

```python
from functools import partial

import jax
import jax.numpy as jnp
from jax import lax
from jax.experimental import pallas as pl
from jax.experimental.pallas import tpu as pltpu
from jax.sharding import PartitionSpec as P

HD = 64
PAIR = 2 * HD
TEXT = 512
NREL = 256
NBOX = 64
BLK = 128
ROWS = 64
EPSILON = 1e-05
MASKED = -1e30
SCALE = HD ** (-0.5)
F32 = jnp.float32
BF16 = jnp.bfloat16
MIB = 1 << 20
VMEM = 18
COST = 0.35e9
FF_STEPS = 3


def mm(a, b):
    return jnp.dot(a, b, preferred_element_type=F32)


def mm_nt(a, b):
    return lax.dot_general(a, b, (((1,), (1,)), ((), ())), preferred_element_type=F32)


def mm_tn(a, b):
    return lax.dot_general(a, b, (((0,), (0,)), ((), ())), preferred_element_type=F32)


MICROS = (
    ("projections", 4.0),
    ("attention_forward", 6.0),
    ("feed_forward_backward", 5.0),
    ("feed_forward", 3.5),
    ("first_norm", 2.0),
    ("visual_attention", 5.0),
    ("text_attention", 5.0),
    ("_part", 2.5),
    ("out_and_visual", 5.0),
    ("spatial_gradients", 2.0),
    ("gradient", 3.0),
)


def micros(name):
    return next((t for key, t in MICROS if key in name), 1.2)


def call(body, name, grid, args, in_specs, outs, out_specs, scratch=(), deps=(), aliases=None):
    aliases = dict(aliases or {})
    n_in, extra = len(args), list(aliases.values()) + list(deps)

    def inner(*refs):
        body(*refs[:n_in], *refs[n_in + len(extra) :])

    return pl.pallas_call(
        inner,
        out_shape=outs,
        grid_spec=pltpu.PrefetchScalarGridSpec(
            num_scalar_prefetch=0,
            grid=grid,
            in_specs=list(in_specs) + [pl.BlockSpec(memory_space=pl.ANY)] * len(extra),
            out_specs=out_specs,
            scratch_shapes=list(scratch),
        ),
        input_output_aliases={n_in + k: out for k, out in enumerate(aliases)},
        compiler_params=pltpu.CompilerParams(
            dimension_semantics=("arbitrary",) * len(grid), vmem_limit_bytes=VMEM * MIB
        ),
        cost_estimate=pl.CostEstimate(flops=int(COST * micros(name)), bytes_accessed=1000, transcendentals=0),
        name=name,
    )(*args, *extra)


def whole(x):
    nd = x.ndim
    return pl.BlockSpec(x.shape, lambda p: (0,) * nd)


def sds(shape, dtype=F32):
    return jax.ShapeDtypeStruct(shape, dtype)


def pair_block(rows, width):
    return pl.BlockSpec((rows, width), lambda p: (0, p))


def lead_block(x):
    nd = x.ndim
    return pl.BlockSpec((1,) + x.shape[1:], lambda p: (p,) + (0,) * (nd - 1))


def proj_body(hid, spa, vis, wt, wv, tb, vb, tqs, tks, tv, vq, vk, vv, hot):
    ph = mm(hid[...], jnp.concatenate([wt[0], wt[1], wt[2], wv[0]], 1)).astype(BF16)
    ps = mm(spa[...], jnp.concatenate([wt[3], wt[4]], 1)).astype(BF16)
    pv = mm(vis[...], jnp.concatenate([wv[1], wv[2]], 1)).astype(BF16)
    scale = jnp.asarray(SCALE, BF16)
    tqs[0, :, :PAIR] = ph[:, :PAIR] * scale
    tqs[0, :, PAIR:] = ps[:, :PAIR] * scale
    tks[0, :, :PAIR] = ph[:, PAIR : 2 * PAIR]
    tks[0, :, PAIR:] = ps[:, PAIR:]
    tv[0] = ph[:, 2 * PAIR : 3 * PAIR]
    vq[0] = ph[:, 3 * PAIR :] * scale
    vk[0] = pv[:, :PAIR]
    vv[0] = pv[:, PAIR:]

    @pl.when(pl.program_id(0) == 0)
    def _():
        row = lax.broadcasted_iota(jnp.int32, (PAIR, hot.shape[1]), 0) % HD
        for k, box in enumerate((tb, vb)):
            hot[k] = jnp.where(row == box[...], 1.0, 0.0).T.astype(BF16)
            hot[k + 2] = jnp.where(row == NBOX - 1 - box[...], 1.0, 0.0).T.astype(BF16)


def projections(hidden, spatial, visual, w_text, w_vis, text_box, vis_box):
    n, d = hidden.shape
    pairs = w_text.shape[2] // PAIR
    wide, slim = sds((pairs, n, 2 * PAIR), BF16), sds((pairs, n, PAIR), BF16)
    outs = [wide, wide, slim, slim, slim, slim]
    hot = sds((4, n, PAIR), BF16)
    args = (hidden, spatial, visual, w_text, w_vis, text_box, vis_box)
    specs = [whole(x) for x in args]
    specs[3] = pl.BlockSpec((5, d, PAIR), lambda p: (0, 0, p))
    specs[4] = pl.BlockSpec((3, d, PAIR), lambda p: (0, 0, p))
    return call(
        proj_body,
        "projections",
        (pairs,),
        args,
        specs,
        outs + [hot],
        [lead_block(o) for o in outs] + [whole(hot)],
    )


def head_mask(h, width):
    lane = lax.broadcasted_iota(jnp.int32, (1, width), 1)
    return jnp.where((lane // HD) % 2 == h, 1.0, 0.0).astype(BF16)


def box_rows(tables, stream, head):
    row = tables[stream, pl.ds(head, 1), :]
    rolled = pltpu.roll(jnp.broadcast_to(row, (NBOX, PAIR)), NBOX, 1, stride=1, stride_axis=0)
    lane = lax.broadcasted_iota(jnp.int32, (NBOX, PAIR), 1)
    rolled = jnp.where(lane < NBOX, rolled, 0.0)
    high = rolled.astype(BF16)
    return jnp.concatenate([high, (rolled - high.astype(F32)).astype(BF16)], 0)


def rel_band(extended_row):
    wide = jnp.broadcast_to(extended_row, (BLK, 4 * BLK))
    return pltpu.roll(wide, 0, 1, stride=1, stride_axis=0)[:, BLK:]


def rel_bias(band, ends, block, blocks, skip):
    pieces = []
    for other in range(blocks):
        step = other - block
        if step >= 2:
            pieces.append(jnp.broadcast_to(ends[1], (ROWS, BLK)))
        elif step <= -2:
            pieces.append(jnp.broadcast_to(ends[0], (ROWS, BLK)))
        else:
            pieces.append(band[skip : skip + ROWS, (step + 1) * BLK : (step + 2) * BLK])
    return jnp.concatenate(pieces, 1)


def rel_parts(rel, head):
    row = rel[pl.ds(head, 1), :]
    ends = (row[:, :1], row[:, NREL - 1 :])
    low, high = (jnp.broadcast_to(e, (1, NREL // 2)) for e in ends)
    return rel_band(jnp.concatenate([low, row, high], 1)), ends


def accumulate(out, term):
    @pl.when(pl.program_id(0) == 0)
    def _():
        out[...] = term

    @pl.when(pl.program_id(0) > 0)
    def _():
        out[...] += term


def accumulate_halves(top, bottom, term):
    half = top.shape[0]
    accumulate(top, term[:half])
    accumulate(bottom, term[half:])


def attend(scores_of, count, probs_ref, values):
    logs = []
    for b in range(count // ROWS):
        scores = scores_of(b)
        peak = jnp.max(scores, 1, keepdims=True)
        powers = jnp.exp(scores - peak)
        total = jnp.sum(powers, 1, keepdims=True)
        probs_ref[b * ROWS : (b + 1) * ROWS, :] = (powers * (1.0 / total)).astype(BF16)
        logs.append(peak + jnp.log(total))
    return mm(probs_ref[...], values), jnp.concatenate(logs, 0)


def forward_body(
    vlen, tqs, vq, tks, tv, vk, vv, hot_q, hot, rel, tables, wo, attn, to, vo, lse, s_ref, p_ref, *, first
):
    count = tqs.shape[1]
    keys_n = tks.shape[1]
    keys_t = jnp.concatenate([tks[0], hot[0]], 1)
    keys_v = jnp.concatenate([vk[0], hot[1]], 1)
    valid = lax.broadcasted_iota(jnp.int32, (1, keys_n), 1) < vlen[0]
    lane = lax.broadcasted_iota(jnp.int32, (count, PAIR), 1)
    text_out, vis_out, logs = [], [], []
    for h in range(2):
        head = 2 * pl.program_id(0) + h
        look_t = mm_nt(hot_q[0], box_rows(tables, 0, head)).astype(BF16)
        look_v = mm_nt(hot_q[0], box_rows(tables, 1, head)).astype(BF16)
        query_t = jnp.concatenate([tqs[0] * head_mask(h, 2 * PAIR), look_t], 1)
        query_v = jnp.concatenate([vq[0] * head_mask(h, PAIR), look_v], 1)
        band, ends = rel_parts(rel, head)
        s_ref[2 * h] = mm_nt(query_t, keys_t)
        s_ref[2 * h + 1] = mm_nt(query_v, keys_v)

        def text_scores(b, h=h, band=band, ends=ends):
            at = first + b * ROWS
            bias = rel_bias(band, ends, at // BLK, keys_n // BLK, at % BLK)
            return s_ref[2 * h, b * ROWS : (b + 1) * ROWS, :] + bias

        def vis_scores(b, h=h):
            return jnp.where(valid, s_ref[2 * h + 1, b * ROWS : (b + 1) * ROWS, :], MASKED)

        out, log = attend(text_scores, count, p_ref.at[2 * h], tv[0])
        text_out.append(out)
        logs.append(log)
        out, log = attend(vis_scores, count, p_ref.at[2 * h + 1], vv[0])
        vis_out.append(out)
        logs.append(log)
    out_t = jnp.where(lane < HD, text_out[0], text_out[1]).astype(BF16)
    out_v = jnp.where(lane < HD, vis_out[0], vis_out[1]).astype(BF16)
    to[...] = out_t
    vo[...] = out_v
    kept = jnp.zeros((count, PAIR), F32)
    for spot, log in zip((0, 2, 1, 3), logs):
        kept = jnp.where(lane == spot, log, kept)
    lse[0] = kept
    term = mm(jnp.concatenate([out_t, out_v], 1), jnp.concatenate([wo[0], wo[1]], 0))

    accumulate(attn, term)


def forward_rows(first, count, proj, vlen, rel, tables, w_out, deps=(), into=None):
    tqs, tks, tv, vq, vk, vv, hot = proj
    pairs, n, _ = tqs.shape
    d = w_out.shape[2]
    spot = first // count

    def rows_of(x):
        return pl.BlockSpec((1, count, x.shape[2]), lambda p: (p, spot, 0))

    return call(
        partial(forward_body, first=first),
        f"attention_forward_{spot}",
        (pairs,),
        (vlen, tqs, vq, tks, tv, vk, vv, hot, hot, rel, tables, w_out),
        [
            pl.BlockSpec(memory_space=pltpu.SMEM),
            rows_of(tqs),
            rows_of(vq),
            lead_block(tks),
            lead_block(tv),
            lead_block(vk),
            lead_block(vv),
            pl.BlockSpec((1, count, PAIR), lambda p: (0, spot, 0)),
            whole(hot),
            whole(rel),
            whole(tables),
            pl.BlockSpec((2, PAIR, d), lambda p: (0, p, 0)),
        ],
        [
            sds((count, d)),
            sds((n, pairs * PAIR), BF16),
            sds((n, pairs * PAIR), BF16),
            sds((pairs, n, PAIR)),
        ],
        [
            pl.BlockSpec((count, d), lambda p: (0, 0)),
            pl.BlockSpec((count, PAIR), lambda p: (spot, p)),
            pl.BlockSpec((count, PAIR), lambda p: (spot, p)),
            pl.BlockSpec((1, count, PAIR), lambda p: (p, spot, 0)),
        ],
        [pltpu.VMEM((4, count, n), F32), pltpu.VMEM((4, count, n), BF16)],
        deps=deps,
        aliases=None if into is None else {1: into[1], 2: into[2], 3: into[3]},
    )


def scores_gradient(probs, grad_probs):
    inner = jnp.sum(grad_probs * probs, 1, keepdims=True)
    return (probs * (grad_probs - inner)).astype(BF16)


def box_gradient(hot, spread, out):
    high = spread.astype(BF16)
    rest = (spread - high.astype(F32)).astype(BF16)
    table = (mm_tn(hot, high) + mm_tn(hot, rest))[:NBOX]
    lane = lax.broadcasted_iota(jnp.int32, (NBOX, PAIR), 1)
    for h in range(2):
        mine = table if h == 0 else pltpu.roll(table, NBOX, 1)
        mine = jnp.where(lane < NBOX, mine, 0.0)
        sheared = pltpu.roll(mine, 1, 1, stride=1, stride_axis=0)
        out[0, h : h + 1, :] = jnp.sum(sheared, 0, keepdims=True)


def shear_sum(band):
    width = band.shape[1]
    rows = BLK
    while rows > 8:
        rows //= 2
        band = band[:rows] + pltpu.roll(band[rows:], width - rows, 1)
    row = lax.broadcasted_iota(jnp.int32, band.shape, 0)
    for bit in (4, 2, 1):
        band = jnp.where((row // bit) % 2 == 1, pltpu.roll(band, width - bit, 1), band)
    return jnp.sum(band, 0, keepdims=True)


def visual_back_body(vlen, vq, vk, vv, dvo, lse, hot_q, hot, tables, *refs, last):
    if last:
        before, wv, dxq, dxv, g_vis, g_box, ds_ref, pb_ref, s_ref, dp_ref = refs
    else:
        dxq, partial_kv, g_box, ds_ref, pb_ref, s_ref, dp_ref = refs
    count = vq.shape[1]
    keys = jnp.concatenate([vk[0], hot[1]], 1)
    valid = lax.broadcasted_iota(jnp.int32, (1, vk.shape[1]), 1) < vlen[0]
    dq = dkt = dvt = spread = None
    for h in range(2):
        mask = head_mask(h, PAIR)
        look = mm_nt(hot_q[0], box_rows(tables, 1, 2 * pl.program_id(0) + h)).astype(BF16)
        mine = vq[0] * mask
        query = jnp.concatenate([mine, look], 1)
        grad = dvo[...] * mask
        s_ref[...] = mm_nt(query, keys)
        dp_ref[...] = mm_nt(grad, vv[0])
        for b in range(count // ROWS):
            part = slice(b * ROWS, (b + 1) * ROWS)
            scores = jnp.where(valid, s_ref[part, :], MASKED)
            probs = jnp.exp(scores - lse[0, part, 2 + h : 3 + h])
            pb_ref[part, :] = probs.astype(BF16)
            ds_ref[part, :] = scores_gradient(probs, dp_ref[part, :])
        ds, pb = ds_ref[...], pb_ref[...]
        terms = (mm(ds, vk[0] * mask), mm_tn(mine, ds), mm_tn(grad, pb), mm(ds, hot[3] * mask))
        if h == 0:
            dq, dkt, dvt, spread = terms
        else:
            dq, dkt, dvt, spread = (a + b for a, b in zip((dq, dkt, dvt, spread), terms))
    box_gradient(hot_q[0], spread, g_box)
    dxq[...] = (dq * SCALE).astype(BF16)
    if last:
        both = jnp.concatenate(
            [(before[0, :PAIR] + dkt).astype(BF16), (before[0, PAIR:] + dvt).astype(BF16)], 0
        ).T
        dxv[...] = both
        accumulate(g_vis, mm_nt(both, jnp.concatenate([wv[1], wv[2]], 1)))
    else:
        partial_kv[0, :PAIR] = dkt
        partial_kv[0, PAIR:] = dvt


def visual_back(spot, proj, vlen, tables, dvo, lse, w_vis, before=None, deps=()):
    vq, vk, vv, hot = proj[3:]
    pairs, n, _ = vq.shape
    d, count = w_vis.shape[1], n // 2
    last = before is not None

    def rows_of(x):
        return pl.BlockSpec((1, count, x.shape[2]), lambda p: (p, spot, 0))

    half = pl.BlockSpec((count, PAIR), lambda p: (spot, p))
    args = (vlen, vq, vk, vv, dvo, lse, hot, hot, tables)
    specs = [
        pl.BlockSpec(memory_space=pltpu.SMEM),
        rows_of(vq),
        lead_block(vk),
        lead_block(vv),
        half,
        rows_of(lse),
        pl.BlockSpec((1, count, PAIR), lambda p: (0, spot, 0)),
        whole(hot),
        whole(tables),
    ]
    box = sds((pairs, 8, PAIR))
    kept = sds((pairs, 2 * PAIR, n))
    outs, out_specs = [sds((n, pairs * PAIR), BF16)], [half]
    if last:
        args += (before[1], w_vis)
        specs += [lead_block(kept), pl.BlockSpec((3, d, PAIR), lambda p: (0, 0, p))]
        outs += [sds((n, pairs * 2 * PAIR), BF16), sds((n, d)), box]
        out_specs += [pair_block(n, 2 * PAIR), pl.BlockSpec((n, d), lambda p: (0, 0)), lead_block(box)]
    else:
        outs += [kept, box]
        out_specs += [lead_block(kept), lead_block(box)]
    return call(
        partial(visual_back_body, last=last),
        f"visual_attention_backward_{spot}",
        (pairs,),
        args,
        specs,
        outs,
        out_specs,
        [pltpu.VMEM((count, n), BF16)] * 2 + [pltpu.VMEM((count, n), F32)] * 2,
        deps=deps,
        aliases={0: before[0]} if last else None,
    )


def text_back_body(
    tqs, tks, tv, dto, lse, hot, rel, tables, dxh, dxs, g_box, g_rel, ds_ref, pb_ref, s_ref, dp_ref, *, pair
):
    n = tqs.shape[1]
    keys = jnp.concatenate([tks[0], hot[0]], 1)
    dq = dkt = dvt = spread = None
    for h in range(2):
        mask, wide_mask = head_mask(h, PAIR), head_mask(h, 2 * PAIR)
        look = mm_nt(hot[0], box_rows(tables, 0, 2 * pair + h)).astype(BF16)
        mine = tqs[0] * wide_mask
        query = jnp.concatenate([mine, look], 1)
        grad = dto[...] * mask
        band, ends = rel_parts(rel, 2 * pair + h)
        near = [None] * 3
        low = high = jnp.zeros((BLK, BLK), F32)
        s_ref[...] = mm_nt(query, keys)
        dp_ref[...] = mm_nt(grad, tv[0])
        for b in range(n // ROWS):
            part = slice(b * ROWS, (b + 1) * ROWS)
            at = b * ROWS
            bias = rel_bias(band, ends, at // BLK, n // BLK, at % BLK)
            probs = jnp.exp(s_ref[part, :] + bias - lse[0, part, h : h + 1])
            pb_ref[part, :] = probs.astype(BF16)
            ds_ref[part, :] = scores_gradient(probs, dp_ref[part, :])
        for b in range(n // BLK):
            ds = ds_ref[b * BLK : (b + 1) * BLK, :].astype(F32)
            for other in range(n // BLK):
                piece = ds[:, other * BLK : (other + 1) * BLK]
                step = other - b
                if step >= 2:
                    high = high + piece
                elif step <= -2:
                    low = low + piece
                else:
                    near[step + 1] = piece if near[step + 1] is None else near[step + 1] + piece
        ds, pb = ds_ref[...], pb_ref[...]
        sums = shear_sum(jnp.concatenate(near + [jnp.zeros((BLK, BLK), F32)], 1))
        far = jnp.concatenate(
            [jnp.sum(low, 0, keepdims=True), jnp.sum(high, 0, keepdims=True)], 1
        )
        g_rel[0, 2 * h : 2 * h + 1, :] = sums
        g_rel[0, 2 * h + 1 : 2 * h + 2, : 2 * BLK] = far
        terms = (mm(ds, tks[0] * wide_mask), mm_tn(mine, ds), mm_tn(grad, pb), mm(ds, hot[2] * mask))
        if h == 0:
            dq, dkt, dvt, spread = terms
        else:
            dq, dkt, dvt, spread = (a + b for a, b in zip((dq, dkt, dvt, spread), terms))
    box_gradient(hot[0], spread, g_box)
    dqs = (dq * SCALE).astype(BF16)
    rest = jnp.concatenate([dkt.astype(BF16), dvt.astype(BF16)], 0).T
    dxs[...] = jnp.concatenate([dqs[:, PAIR:], rest[:, PAIR : 2 * PAIR]], 1)
    dxh[...] = jnp.concatenate([dqs[:, :PAIR], rest[:, :PAIR], rest[:, 2 * PAIR :]], 1)


def text_back(pair, proj, rel, tables, dto, lse, into=None, deps=()):
    tqs, tks, tv = proj[:3]
    hot = proj[6]
    pairs, n, _ = tqs.shape

    def lead(x):
        return pl.BlockSpec((1,) + x.shape[1:], lambda p: (pair, 0, 0))

    def block(width):
        return pl.BlockSpec((n, width), lambda p: (0, pair))

    outs = [
        sds((n, pairs * 3 * PAIR), BF16),
        sds((n, pairs * 2 * PAIR), BF16),
        sds((pairs, 8, PAIR)),
        sds((pairs, 8, 4 * BLK)),
    ]
    return call(
        partial(text_back_body, pair=pair),
        f"text_attention_backward_{pair}",
        (1,),
        (tqs, tks, tv, dto, lse, hot, rel, tables),
        [lead(tqs), lead(tks), lead(tv), block(PAIR), lead(lse), whole(hot), whole(rel), whole(tables)],
        outs,
        [block(3 * PAIR), block(2 * PAIR), lead(outs[2]), lead(outs[3])],
        [pltpu.VMEM((n, n), BF16)] * 2 + [pltpu.VMEM((n, n), F32)] * 2,
        deps=deps,
        aliases=None if into is None else {k: into[k] for k in range(4)},
    )


def spatial_part_body(dxs, wt, out):
    accumulate(out, mm_nt(dxs[...], jnp.concatenate([wt[3], wt[4]], 1)))


def spatial_part(dxs, w_text, deps=()):
    n, d = dxs.shape[0], w_text.shape[1]
    return call(
        spatial_part_body,
        "spatial_part",
        (dxs.shape[1] // (2 * PAIR),),
        (dxs, w_text),
        [pair_block(n, 2 * PAIR), pl.BlockSpec((5, d, PAIR), lambda p: (0, 0, p))],
        sds((n, d)),
        pl.BlockSpec((n, d), lambda p: (0, 0)),
        deps=deps,
    )


def hidden_part_body(dxh, dxq, wt, wv, top, bottom):
    accumulate_halves(
        top,
        bottom,
        mm_nt(
            jnp.concatenate([dxh[...], dxq[...]], 1), jnp.concatenate([wt[0], wt[1], wt[2], wv[0]], 1)
        ),
    )


def hidden_part(dxh, dxq, w_text, w_vis, deps=()):
    n, d = dxh.shape[0], w_text.shape[1]
    half = pl.BlockSpec((n // 2, d), lambda p: (0, 0))
    return call(
        hidden_part_body,
        "hidden_part",
        (dxq.shape[1] // PAIR,),
        (dxh, dxq, w_text, w_vis),
        [
            pair_block(n, 3 * PAIR),
            pair_block(n, PAIR),
            pl.BlockSpec((5, d, PAIR), lambda p: (0, 0, p)),
            pl.BlockSpec((3, d, PAIR), lambda p: (0, 0, p)),
        ],
        [sds((n // 2, d))] * 2,
        [half] * 2,
        deps=deps,
    )


def normalise(values):
    centred = values - jnp.mean(values, 1, keepdims=True)
    rstd = lax.rsqrt(jnp.mean(centred * centred, 1, keepdims=True) + EPSILON)
    return centred * rstd, rstd


def norm_back(grad, unit, rstd, gain):
    scaled = grad * gain
    mean_one = jnp.mean(scaled, 1, keepdims=True)
    mean_two = jnp.mean(scaled * unit, 1, keepdims=True)
    return rstd * (scaled - mean_one - unit * mean_two)


def column_sum(x):
    return jnp.sum(x, 0, keepdims=True)


def up_body(hid, own, got, gain, bias, w_up, b_up, w_down, h1b, z, r1, h1, slope, f):
    @pl.when(pl.program_id(0) == 0)
    def _():
        total = hid[...].astype(F32) + (own[...] + got[...])
        unit, _ = normalise(total)
        normed = unit * gain[0:1, :] + bias[0:1, :]
        r1[...] = total
        h1[...] = normed
        h1b[...] = normed.astype(BF16)

    u = mm(h1b[...], w_up[...]) + b_up[...]
    cdf = 0.5 * (1.0 + lax.erf(u * (0.5**0.5)))
    slope[...] = cdf + u * (jnp.exp(-0.5 * u * u) * 0.3989422804014327)
    active = (u * cdf).astype(BF16)
    z[...] = active
    accumulate(f, mm(active, w_down[...]))


def row_call(body, name, spot, grid, args, specs, outs, out_specs, halved, deps, into):
    return call(
        body,
        f"{name}_{spot}",
        grid,
        args,
        specs,
        outs,
        out_specs,
        deps=deps,
        aliases=None if into is None else {k: into[k] for k in halved},
    )


def up_rows(spot, hidden, own, got, gain, bias, w_up, b_up, w_down, deps=(), into=None):
    n, d = hidden.shape
    ff = w_up.shape[1]
    count, block = n // 2, ff // FF_STEPS
    half = pl.BlockSpec((count, d), lambda p: (spot, 0))
    own_half = pl.BlockSpec((count, d), lambda p: (0, 0))
    args = (hidden, own, got, gain, bias, w_up, b_up, w_down)
    specs = [half, own_half, own_half, whole(gain), whole(bias), pair_block(d, block)]
    specs += [pair_block(1, block), pl.BlockSpec((block, d), lambda p: (p, 0))]
    outs = [sds((n, d), BF16), sds((n, ff), BF16), sds((count, d)), sds((count, d))]
    outs += [sds((count, ff)), sds((count, d))]
    out_specs = [half, pl.BlockSpec((count, block), lambda p: (spot, p)), own_half, own_half]
    out_specs += [pair_block(count, block), own_half]
    return row_call(up_body, "feed_forward", spot, (FF_STEPS,), args, specs, outs, out_specs, (0, 1), deps, into)


def down_body(
    h1, own, got, cot, gain, bias, b_down, w_down, w_up, slope, result, df, du, dr2, pd, sums, sum_up
):
    @pl.when(pl.program_id(0) == 0)
    def _():
        total = h1[...] + ((own[...] + got[...]) + b_down[...])
        unit, rstd = normalise(total)
        result[...] = (unit * gain[1:2, :] + bias[1:2, :]).astype(BF16)
        grad = cot[...].astype(F32)
        back = norm_back(grad, unit, rstd, gain[1:2, :])
        low = back.astype(BF16)
        dr2[...] = back
        df[...] = low
        sums[0:1, :] = column_sum(grad * unit)
        sums[1:2, :] = column_sum(grad)
        sums[2:3, :] = column_sum(low.astype(F32))

    grad_u = (slope[...] * mm_nt(df[...], w_down[...])).astype(BF16)
    du[...] = grad_u
    sum_up[0:1, :] = column_sum(grad_u.astype(F32))
    accumulate(pd, mm_nt(grad_u, w_up[...]))


def down_rows(spot, h1, own, got, cotangent, gain, bias, b_down, w_down, w_up, slope, deps=(), into=None):
    n, d = cotangent.shape
    ff = w_up.shape[1]
    count, block = n // 2, ff // FF_STEPS
    half = pl.BlockSpec((count, d), lambda p: (spot, 0))
    own_half = pl.BlockSpec((count, d), lambda p: (0, 0))
    args = (h1, own, got, cotangent, gain, bias, b_down, w_down, w_up, slope)
    specs = [own_half] * 3 + [half, whole(gain), whole(bias), whole(b_down)]
    specs += [pl.BlockSpec((block, d), lambda p: (p, 0)), pair_block(d, block), pair_block(count, block)]
    outs = [sds((n, d), BF16), sds((n, d), BF16), sds((n, ff), BF16), sds((count, d))]
    outs += [sds((count, d)), sds((8, d)), sds((8, ff))]
    out_specs = [half, half, pl.BlockSpec((count, block), lambda p: (spot, p)), own_half, own_half]
    out_specs += [whole(outs[5]), pair_block(8, block)]
    return row_call(
        down_body, "feed_forward_backward", spot, (FF_STEPS,), args, specs, outs, out_specs, (0, 1, 2), deps, into
    )


def first_body(dr2, own, got, r1, gain, w_out, dr1, da, dto, dvo, sums):
    grad = dr2[...] + (own[...] + got[...])
    unit, rstd = normalise(r1[...])
    back = norm_back(grad, unit, rstd, gain[0:1, :])
    low = back.astype(BF16)
    dr1[...] = back
    da[...] = low
    dto[...] = mm_nt(low, w_out[0]).astype(BF16)
    dvo[...] = mm_nt(low, w_out[1]).astype(BF16)
    sums[0:1, :] = column_sum(grad * unit)
    sums[1:2, :] = column_sum(grad)


def first_rows(spot, dr2, own, got, r1, gain, w_out, deps=(), into=None):
    n, d = 2 * own.shape[0], own.shape[1]
    width = w_out.shape[1]
    args = (dr2, own, got, r1, gain, w_out)
    outs = [sds((n, d)), sds((n, d), BF16)]
    outs += [sds((n, width), BF16), sds((n, width), BF16), sds((8, d))]
    out_specs = [pl.BlockSpec((n // 2, x.shape[1]), lambda p: (spot, 0)) for x in outs[:4]] + [whole(outs[4])]
    return row_call(
        first_body,
        "first_norm_backward",
        spot,
        (1,),
        args,
        [whole(x) for x in args],
        outs,
        out_specs,
        (0, 1, 2, 3),
        deps,
        into,
    )


def pack_body(one_a, one_b, two_a, two_b, up_a, up_b, g_rel, g_box_t, g_box_v, g_box_w, out):
    d = out.shape[1]
    one = one_a[...] + one_b[...]
    two = two_a[...] + two_b[...]
    up = up_a[...] + up_b[...]
    out[...] = jnp.zeros(out.shape, F32)
    out[0:1, :] = one[0:1]
    out[1:2, :] = two[0:1]
    out[2:3, :] = one[1:2]
    out[3:4, :] = two[1:2]
    out[4:5, :] = two[2:3]
    out[5:6, :] = up[0:1, :d]
    out[6:7, :] = up[0:1, d:]
    half = NREL // 2
    lane = lax.broadcasted_iota(jnp.int32, (1, 2 * NREL), 1)
    for head in range(2 * g_rel.shape[0]):
        p, h = head // 2, head % 2
        near = g_rel[p, 2 * h : 2 * h + 1, :]
        far = g_rel[p, 2 * h + 1 : 2 * h + 2, :NREL]
        low = jnp.sum(jnp.where((lane > 3 * half) | (lane == 0), near, 0.0), 1, keepdims=True)
        low = low + jnp.sum(far[:, :half], 1, keepdims=True)
        high = jnp.sum(jnp.where((lane >= 2 * half - 1) & (lane < 3 * half), near, 0.0), 1, keepdims=True)
        high = high + jnp.sum(far[:, half:], 1, keepdims=True)
        short = lane[:, :NREL]
        row = jnp.where(short == 0, low, jnp.where(short == NREL - 1, high, near[:, :NREL]))
        spot = 8 + head
        out[spot : spot + 1, :NREL] = row
        out[spot : spot + 1, NREL : NREL + PAIR] = g_box_t[p, h : h + 1, :]
        out[spot : spot + 1, NREL + PAIR : NREL + 2 * PAIR] = (
            g_box_v[p, h : h + 1, :] + g_box_w[p, h : h + 1, :]
        )


def pack_small(d, args, deps=()):
    heads = 2 * args[6].shape[0]
    out = sds((8 + -(-heads // 8) * 8, d))
    return call(
        pack_body, "small_pack", (1,), args, [whole(x) for x in args], out, whole(out), deps=deps
    )


def unpack_body(own, rel, space, gain, bias, b_up, b_down):
    x = own[...]
    d = x.shape[1]
    gain[...] = x[0:2]
    bias[...] = x[2:4]
    b_down[...] = x[4:5]
    b_up[:, :d] = x[5:6]
    b_up[:, d:] = x[6:7]
    heads = rel.shape[0]
    rel[...] = x[8 : 8 + heads, :NREL]
    space[0] = x[8 : 8 + heads, NREL : NREL + PAIR]
    space[1] = x[8 : 8 + heads, NREL + PAIR : NREL + 2 * PAIR]


def unpack_small(own, heads, ff, deps=()):
    d = own.shape[1]
    outs = [sds((heads, NREL)), sds((2, heads, PAIR)), sds((2, d)), sds((2, d)), sds((1, ff)), sds((1, d))]
    return call(
        unpack_body, "small_unpack", (1,), (own,), [whole(own)], outs, [whole(x) for x in outs], deps=deps
    )


def product_body(order, *refs, sets, chunk):
    count = sum(1 + len(widths) for widths in sets)
    ins, mine = refs[:count], refs[count]
    scratch = refs[len(refs) - 2 * len(sets) :]
    others = refs[count + 1 : len(refs) - 2 * len(sets)]
    half = mine.shape[0]
    p = pl.program_id(0)
    at = column = 0
    for k, widths in enumerate(sets):
        left, cols = ins[at], ins[at + 1 : at + 1 + len(widths)]
        at += 1 + len(widths)
        plain, placed = scratch[2 * k : 2 * k + 2]

        @pl.when(pl.program_id(0) == 0)
        def _():
            if chunk is None:
                placed[...] = left[...].T
            else:
                plain[...] = left[...].T
                for r in range(plain.shape[0] // chunk):
                    spot = pl.multiple_of(order[r] * chunk, chunk)
                    placed[r * chunk : (r + 1) * chunk, :] = plain[pl.ds(spot, chunk), :]

        right = jnp.concatenate([c[...] for c in cols], 1) if len(cols) > 1 else cols[0][...]
        out = mm(placed[...], right)
        end = column + sum(widths)
        mine[:, column:end] = out[:half]
        for step, other in enumerate(others):

            @pl.when(p == step)
            def _(other=other, out=out, column=column, end=end):
                other[:, column:end] = out[half:]

        column = end


def weight_product(name, links, sets, deps=()):
    n, d = sets[0][0].shape
    chunk = d // links.n
    args, specs = [links.order()], [pl.BlockSpec(memory_space=pltpu.SMEM)]
    for rows, cols, widths in sets:
        if chunk % 16:
            rows = jnp.take(rows.reshape(n, links.n, chunk), links.order(), axis=1, mode="clip").reshape(n, d)
        args += [rows, *cols]
        specs += [whole(rows)] + [pair_block(n, w) for w in widths]
    steps = sets[0][1][0].shape[1] // sets[0][2][0]
    total = sum(sum(widths) for _, _, widths in sets)
    return call(
        partial(product_body, sets=[w for _, _, w in sets], chunk=None if chunk % 16 else chunk),
        name,
        (steps,),
        tuple(args),
        specs,
        [sds((d // 2, steps * total))] + [sds((d // 2, total))] * steps,
        [pair_block(d // 2, total)] + [pl.BlockSpec((d // 2, total), lambda p: (0, 0))] * steps,
        [pltpu.VMEM((d, n), BF16)] * (2 * len(sets)),
        deps=deps,
    )


def flat(terms):
    return [x for arrays, _, _ in terms for x in arrays]


def sum_terms(refs, counts):
    total, at = None, 0
    for count in counts:
        pieces = [ref[...] for ref in refs[at : at + count]]
        at += count
        value = pieces[0] if count == 1 else jnp.concatenate(pieces, 1)
        total = value if total is None else total + value
    return total


def add_body(*refs, counts):
    refs[-1][...] = sum_terms(refs[:-1], counts)


def add_chunks(name, terms, rows, blocks, deps=()):
    width = sum(x.shape[1] for x in terms[0][0])
    if rows % 8:
        out = []
        for k in range(blocks):
            pieces = [
                jnp.concatenate([x[(a + k * s) * rows : (a + k * s + 1) * rows] for x in arrays], 1)
                for arrays, a, s in terms
            ]
            out.append(sum(pieces[1:], pieces[0]))
        return jnp.concatenate(out, 0)
    specs = [
        pl.BlockSpec((rows, x.shape[1]), lambda p, a=a, s=s: (a + s * p, 0)) for arrays, a, s in terms for x in arrays
    ]
    return call(
        partial(add_body, counts=[len(arrays) for arrays, _, _ in terms]),
        name,
        (blocks,),
        tuple(flat(terms)),
        specs,
        sds((blocks * rows, width)),
        pl.BlockSpec((rows, width), lambda p: (p, 0)),
        deps=deps,
    )


def total_body(*refs):
    *first, own, got, out = refs
    total = own[...] + got[...]
    for ref in first:
        total = ref[...] + total
    out[...] = total.astype(out.dtype)


def total_rows(name, spot, own, got, dtype, first=(), deps=(), into=None, parts=2):
    count, d = own.shape
    steps = 4 // parts
    block = pl.BlockSpec((count // steps, d), lambda p: (p, 0))
    placed = pl.BlockSpec((count // steps, d), lambda p: (steps * spot + p, 0))
    return call(
        total_body,
        f"{name}_{spot}",
        (steps,),
        (*first, own, got),
        [placed] * len(first) + [block, block],
        sds((parts * count, d), dtype),
        placed,
        deps=deps,
        aliases=None if into is None else {0: into},
    )


def add_small(x, y, deps=()):
    return call(
        partial(add_body, counts=[1, 1]), "small_sum", (1,), (x, y), [whole(x)] * 2, sds(x.shape), whole(x), deps=deps
    )


class Links:
    def __init__(self, sizes):
        self.n = n = sizes["dp"]
        self.core = [(d, d ^ 1) for d in range(n)]
        self.side = [(d, d ^ 2) for d in range(n)]
        self.ring = [(d, (d + 4) % n) for d in range(n)]
        self.turns = n // 4

    def order(self):
        me = lax.axis_index("dp")
        core, side, ring = me % 2, (me // 2) % 2, me // 4
        places = []
        for c in range(2):
            for s in range(2):
                for r in range(self.turns):
                    places.append(((ring + r) % self.turns) * 4 + (side ^ s) * 2 + (core ^ c))
        return jnp.stack(places).astype(jnp.int32)

    def across(self, x):
        return lax.ppermute(x, "tensor", [(0, 1), (1, 0)])

    def move(self, x, how):
        return lax.ppermute(x, "dp", how)


class Scatter:
    def __init__(self, name, links, halves, side_first):
        self.name, self.links, self.side_first = name, links, side_first
        mine, *others = halves
        self.rows = mine.shape[0] // (2 * links.turns)
        self.both = [(mine,), tuple(links.move(other, links.core) for other in others)]
        self.stage = 0

    def done(self):
        return self.stage == self.links.turns

    def step(self, deps=()):
        links, rows, turns, stage = self.links, self.rows, self.links.turns, self.stage
        name = f"{self.name}_{stage}"
        self.stage += 1
        if self.side_first:
            if stage == 0:
                out = add_chunks(name, [(x, turns, 1) for x in self.both], rows, turns, deps)
                self.both.append((links.move(out, links.side),))
                self.terms = [(x, 0, 1) for x in self.both]
                return out
            terms = [(x, turns - stage, 1) for x in self.both]
            if stage > 1:
                terms.append((self.moving, 0, 1))
            out = add_chunks(name, terms, rows, 1, deps)
            self.moving = (links.move(out, links.ring),)
            self.terms = [(x, 0, 1) for x in self.both] + [(self.moving, 0, 1)]
            return out
        if stage < turns - 1:
            terms = [(x, turns - 1 - stage, turns) for x in self.both]
            if stage > 0:
                terms.append((self.moving, 0, 1))
            out = add_chunks(name, terms, rows, 2, deps)
            self.moving = (links.move(out, links.ring),)
            return out
        terms = [(x, turns, 1) for x in self.both] + [(self.moving, 1, 1)]
        out = add_chunks(name, terms, rows, 1, deps)
        self.terms = [(x, 0, 1) for x in self.both] + [(self.moving, 0, 1), ((links.move(out, links.side),), 0, 1)]
        return out

    def rest(self, deps=()):
        while not self.done():
            deps = (self.step(deps),)
        return deps

    def total(self, deps=()):
        deps = self.rest(deps)
        return add_chunks(f"{self.name}_total", self.terms, self.rows, 1, deps)


def spread_body(*refs, counts, places, outs):
    groups = [sum(c) for c in counts]
    ins, out_refs = refs[: sum(groups)], refs[sum(groups) :]
    at = 0
    for count, place in zip(counts, places):
        total = sum_terms(ins[at : at + sum(count)], count)
        at += sum(count)
        width = len(place) * PAIR
        for p in range(total.shape[1] // width):
            for k, (out, m) in enumerate(place):
                block = total[:, p * width + k * PAIR : p * width + (k + 1) * PAIR]
                out_refs[out][m, :, p * PAIR : (p + 1) * PAIR] = block


def spread(name, scatters, places, outs, deps=()):
    rows = scatters[0].rows
    for s in scatters:
        deps = s.rest(deps)
    if rows % 8:
        parts = {}
        for s, place in zip(scatters, places):
            total = s.total(deps).reshape(rows, -1, len(place), PAIR)
            for k, key in enumerate(place):
                parts[key] = total[:, :, k].reshape(rows, -1)
        return [jnp.stack([parts[o, m] for m in range(x.shape[0])]) for o, x in enumerate(outs)]
    args = [x for s in scatters for x in flat(s.terms)]
    return call(
        partial(
            spread_body, counts=[[len(t[0]) for t in s.terms] for s in scatters], places=places, outs=outs
        ),
        name,
        (1,),
        tuple(args),
        [pl.BlockSpec((rows, x.shape[1]), lambda p: (0, 0)) for x in args],
        outs,
        [whole(x) for x in outs],
        deps=deps,
    )


def on_device(
    links,
    hidden,
    spatial,
    visual,
    vis_len,
    text_box,
    vis_box,
    text_weight_matrix,
    w_vis,
    w_out,
    rel_table,
    space_tables,
    norm_gain,
    norm_bias,
    w_up,
    b_up,
    w_down,
    b_down,
    cotangent,
):
    n, d = hidden.shape
    width = w_vis.shape[2]
    pairs = width // PAIR
    ff = w_up.shape[1]
    heads = rel_table.shape[0]
    text_row, vis_row = text_box.reshape(1, n), vis_box.reshape(1, -1)
    b_up_row, b_down_row = b_up.reshape(1, ff), b_down.reshape(1, d)

    proj = projections(hidden, spatial, visual, text_weight_matrix, w_vis, text_row, vis_row)
    count = n // 2
    common = (proj, vis_len, rel_table, space_tables, w_out)
    front_a = forward_rows(0, count, *common)
    got_a = links.across(front_a[0])
    front_b = forward_rows(count, count, *common, deps=(front_a[0],), into=front_a)
    got_b = links.across(front_b[0])
    merged_t, merged_v, lse = front_b[1:]

    feed = (norm_gain, norm_bias, w_up, b_up_row, w_down)
    up_a = up_rows(0, hidden, front_a[0], got_a, *feed, deps=(front_b[0],))
    got_a = links.across(up_a[5])
    up_b = up_rows(1, hidden, front_b[0], got_b, *feed, deps=(up_a[5],), into=up_a)
    got_b = links.across(up_b[5])
    h1_low, active = up_b[:2]

    feed = (cotangent, norm_gain, norm_bias, b_down_row, w_down, w_up)
    down_a = down_rows(0, up_a[3], up_a[5], got_a, *feed, up_a[4], deps=(up_b[5],))
    got_a = links.across(down_a[4])
    down_b = down_rows(1, up_b[3], up_b[5], got_b, *feed, up_b[4], deps=(down_a[4],), into=down_a)
    got_b = links.across(down_b[4])
    result, df, du = down_b[:3]

    first_a = first_rows(0, down_a[3], down_a[4], got_a, up_a[2], norm_gain, w_out, deps=(down_b[4],))
    third = ff // 3
    half_down = weight_product("down_gradient", links, [(df, (active,), (third,))], (first_a[4],))
    sc_down = Scatter("down_sum", links, half_down, True)
    half_up = weight_product("up_gradient", links, [(h1_low, (du,), (third,))], half_down[:1])
    sc_up = Scatter("up_sum", links, half_up, False)
    vis_a = visual_back(
        0, proj, vis_len, space_tables, first_a[3], lse, w_vis, deps=half_up[:1]
    )
    first_b = first_rows(
        1, down_b[3], down_b[4], got_b, up_b[2], norm_gain, w_out, deps=vis_a[1:2], into=first_a
    )
    dr1, da, dto, dvo = first_b[:4]
    last = sc_down.step((first_b[4],))
    last = sc_up.step((last,))
    dxq, dxv, part_vis, g_box_vis = visual_back(
        1, proj, vis_len, space_tables, dvo, lse, w_vis, before=vis_a, deps=(last,)
    )
    got_vis = links.across(part_vis)
    half_mixed = weight_product(
        "out_and_visual_gradients",
        links,
        [(da, (merged_t, merged_v), (PAIR, PAIR)), (visual, (dxv,), (2 * PAIR,))],
        (part_vis,),
    )
    sc_mixed = Scatter("mixed_sum", links, half_mixed, True)
    last = sc_up.step(half_mixed[:1])
    text = text_back(0, proj, rel_table, space_tables, dto, lse, None, (last,))
    last = sc_mixed.step((text[2],))
    last = sc_down.step((last,))
    text = text_back(1, proj, rel_table, space_tables, dto, lse, text, (last,))
    last = sc_up.step((text[2],))
    last = sc_down.step((last,))
    dxh, dxs, g_box_text, g_rel = text_back(2, proj, rel_table, space_tables, dto, lse, text, (last,))
    part_spa = spatial_part(dxs, text_weight_matrix, (g_rel,))
    got_spa = links.across(part_spa)
    half_hid = weight_product(
        "hidden_gradients", links, [(hidden, (dxh, dxq), (3 * PAIR, PAIR))], (part_spa,)
    )
    sc_hid = Scatter("hidden_sum", links, half_hid, True)
    last = grad_visual = total_rows("visual_total", 0, part_vis, got_vis, F32, deps=half_hid[:1], parts=1)
    last = sc_up.step((last,))
    last = sc_mixed.step((last,))
    last = sc_hid.step((last,))
    last = sc_down.step((last,))
    half_spa = weight_product("spatial_gradients", links, [(spatial, (dxs,), (2 * PAIR,))], (last,))
    sc_spa = Scatter("spatial_sum", links, half_spa, True)
    hid_a, hid_b = hidden_part(dxh, dxq, text_weight_matrix, w_vis, half_spa[:1])
    got_a, got_b = links.across(hid_a), links.across(hid_b)
    last = small = pack_small(
        d,
        (first_a[4], first_b[4], down_a[5], down_b[5], down_a[6], down_b[6])
        + (g_rel, g_box_text, vis_a[2], g_box_vis),
        (hid_b,),
    )
    pairs_of = []
    step = links.n // 2
    while step:
        pairs_of.append([(x, x ^ step) for x in range(links.n)])
        step //= 2
    pairs_of = pairs_of[-1:] + pairs_of[:-1]

    def small_step(x, deps):
        return add_small(x, links.move(x, pairs_of.pop(0)), deps)

    last = sc_mixed.step((last,))
    last = small = small_step(small, (last,))
    last = g_w_down = sc_down.total((last,))
    last = sc_mixed.step((last,))
    last = sc_spa.step((last,))
    while len(pairs_of) > 1:
        last = small = small_step(small, (last,))
    last = g_w_up = sc_up.total((last,))
    rows = d // links.n
    matrices = sds((2, rows, width))
    (last,) = sc_mixed.rest((last,))
    last = grad_spatial = total_rows("spatial_total", 0, part_spa, got_spa, F32, deps=(last,), parts=1)
    g_w_out, g_vis = spread(
        "mixed_total", [sc_mixed], [[(0, 0), (0, 1), (1, 0), (1, 1)]], [matrices, matrices], (last,)
    )
    last = sc_hid.step((g_vis,))
    last = sc_hid.step((last,))
    last = sc_hid.step((last,))
    last = sc_spa.step((last,))
    last = small = small_step(small, (last,))
    (last,) = sc_hid.rest((last,))
    last = grad_hidden = total_rows("hidden_total", 0, hid_a, got_a, BF16, (dr1,), deps=(last,))
    (last,) = sc_spa.rest((last,))
    g_hid, g_spa = spread(
        "attention_total",
        [sc_hid, sc_spa],
        [[(0, 0), (0, 1), (0, 2), (0, 3)], [(1, 0), (1, 1)]],
        [sds((4, rows, width)), sds((2, rows, width))],
        (last,),
    )
    grad_hidden = total_rows("hidden_total", 1, hid_b, got_b, BF16, (dr1,), deps=(g_spa,), into=grad_hidden)
    g_rel_table, g_space, g_gain, g_bias, g_b_up, g_b_down = unpack_small(
        small, rel_table.shape[0], ff, (g_spa,)
    )
    g_w_text = jnp.concatenate([g_hid[:3], g_spa], 0)
    g_w_vis = jnp.concatenate([g_hid[3:], g_vis], 0)
    return (
        result,
        grad_hidden,
        grad_spatial,
        grad_visual,
        g_w_text,
        g_w_vis,
        g_w_out.transpose(0, 2, 1),
        g_rel_table,
        g_space,
        g_gain,
        g_bias,
        g_w_up,
        g_b_up.reshape(ff),
        g_w_down.T,
        g_b_down.reshape(d),
    )


def solution(mesh):
    return jax.shard_map(
        partial(on_device, Links(dict(mesh.shape))),
        mesh=mesh,
        in_specs=(
            P("dp", None),
            P("dp", None),
            P("dp", None),
            P("dp"),
            P("dp"),
            P("dp"),
            P(None, None, "tensor"),
            P(None, None, "tensor"),
            P(None, "tensor", None),
            P("tensor", None),
            P(None, "tensor", None),
            P(),
            P(),
            P(None, "tensor"),
            P("tensor"),
            P("tensor", None),
            P(),
            P("dp", None),
        ),
        out_specs=(
            P("dp", None),
            P("dp", None),
            P("dp", None),
            P("dp", None),
            P(None, "dp", "tensor"),
            P(None, "dp", "tensor"),
            P(None, "tensor", "dp"),
            P("tensor", None),
            P(None, "tensor", None),
            P(),
            P(),
            P("dp", "tensor"),
            P("tensor"),
            P("tensor", "dp"),
            P(),
        ),
        check_vma=False,
    )
```

```python
from functools import partial

import jax
import jax.numpy as jnp
from jax import lax
from jax.experimental import pallas as pl
from jax.experimental.pallas import tpu as pltpu
from jax.sharding import PartitionSpec as P

HD = 64
PAIR = 2 * HD
TEXT = 512
NREL = 256
NBOX = 64
BLK = 128
ROWS = 64
EPSILON = 1e-05
MASKED = -1e30
SCALE = HD ** (-0.5)
F32 = jnp.float32
BF16 = jnp.bfloat16
MIB = 1 << 20
VMEM = 18
COST = 0.35e9
FF_STEPS = 3


def mm(a, b):
    return jnp.dot(a, b, preferred_element_type=F32)


def mm_nt(a, b):
    return lax.dot_general(a, b, (((1,), (1,)), ((), ())), preferred_element_type=F32)


def mm_tn(a, b):
    return lax.dot_general(a, b, (((0,), (0,)), ((), ())), preferred_element_type=F32)


STARTS = (
    0.0, 4.0, 10.0, 36.0, 53.0, 70.0, 87.0, 95.0, 98.5, 104.5, 118.5, 119.5,
    120.5, 126.5, 128.0, 131.0, 134.0, 137.0, 138.5, 140.0, 144.0, 146.0, 150.0, 154.0,
    155.5, 158.0, 159.5, 161.0, 171.5, 173.5, 178.0, 179.5, 181.0, 188.5, 192.0, 194.0,
    198.0, 205.0, 207.0, 209.0, 210.0, 211.0, 213.0, 215.0, 222.0, 228.0, 229.0, 230.0,
    232.0, 233.0,
)


class Plan:
    left = []

    @classmethod
    def begin(cls):
        cls.left = [b - a for a, b in zip(STARTS, STARTS[1:])]

    @classmethod
    def weight(cls):
        return cls.left.pop(0) if cls.left else 1.0


def call(body, name, grid, args, in_specs, outs, out_specs, scratch=(), deps=(), aliases=None, far=(), far_in=()):
    aliases = dict(aliases or {})
    if far:
        outs = [pltpu.HBM(o.shape, o.dtype) if k in far else o for k, o in enumerate(outs)]
    args = [pltpu.with_memory_space_constraint(x, pltpu.HBM) if k in far_in else x for k, x in enumerate(args)]
    n_in, extra = len(args), list(aliases.values()) + list(deps)

    def inner(*refs):
        body(*refs[:n_in], *refs[n_in + len(extra) :])

    return pl.pallas_call(
        inner,
        out_shape=outs,
        grid_spec=pltpu.PrefetchScalarGridSpec(
            num_scalar_prefetch=0,
            grid=grid,
            in_specs=list(in_specs) + [pl.BlockSpec(memory_space=pl.ANY)] * len(extra),
            out_specs=out_specs,
            scratch_shapes=list(scratch),
        ),
        input_output_aliases={n_in + k: out for k, out in enumerate(aliases)},
        compiler_params=pltpu.CompilerParams(
            dimension_semantics=("arbitrary",) * len(grid), vmem_limit_bytes=VMEM * MIB
        ),
        cost_estimate=pl.CostEstimate(flops=int(COST * Plan.weight()), bytes_accessed=1000, transcendentals=0),
        name=name,
    )(*args, *extra)


def whole(x):
    nd = x.ndim
    return pl.BlockSpec(x.shape, lambda p: (0,) * nd)


def sds(shape, dtype=F32):
    return jax.ShapeDtypeStruct(shape, dtype)


def pair_block(rows, width):
    return pl.BlockSpec((rows, width), lambda p: (0, p))


def lead_block(x):
    nd = x.ndim
    return pl.BlockSpec((1,) + x.shape[1:], lambda p: (p,) + (0,) * (nd - 1))


def proj_body(hid, spa, vis, wt, wv, tb, vb, tqs, tks, tv, vq, vk, vv, hot):
    ph = mm(hid[...], jnp.concatenate([wt[0], wt[1], wt[2], wv[0]], 1)).astype(BF16)
    ps = mm(spa[...], jnp.concatenate([wt[3], wt[4]], 1)).astype(BF16)
    pv = mm(vis[...], jnp.concatenate([wv[1], wv[2]], 1)).astype(BF16)
    scale = jnp.asarray(SCALE, BF16)
    tqs[0, :, :PAIR] = ph[:, :PAIR] * scale
    tqs[0, :, PAIR:] = ps[:, :PAIR] * scale
    tks[0, :, :PAIR] = ph[:, PAIR : 2 * PAIR]
    tks[0, :, PAIR:] = ps[:, PAIR:]
    tv[0] = ph[:, 2 * PAIR : 3 * PAIR]
    vq[0] = ph[:, 3 * PAIR :] * scale
    vk[0] = pv[:, :PAIR]
    vv[0] = pv[:, PAIR:]

    @pl.when(pl.program_id(0) == 0)
    def _():
        row = lax.broadcasted_iota(jnp.int32, (PAIR, hot.shape[1]), 0) % HD
        for k, box in enumerate((tb, vb)):
            hot[k] = jnp.where(row == box[...], 1.0, 0.0).T.astype(BF16)
            hot[k + 2] = jnp.where(row == NBOX - 1 - box[...], 1.0, 0.0).T.astype(BF16)


def projections(hidden, spatial, visual, w_text, w_vis, text_box, vis_box):
    n, d = hidden.shape
    pairs = w_text.shape[2] // PAIR
    wide, slim = sds((pairs, n, 2 * PAIR), BF16), sds((pairs, n, PAIR), BF16)
    outs = [wide, wide, slim, slim, slim, slim]
    hot = sds((4, n, PAIR), BF16)
    args = (hidden, spatial, visual, w_text, w_vis, text_box, vis_box)
    specs = [whole(x) for x in args]
    specs[3] = pl.BlockSpec((5, d, PAIR), lambda p: (0, 0, p))
    specs[4] = pl.BlockSpec((3, d, PAIR), lambda p: (0, 0, p))
    return call(
        proj_body,
        "P",
        (pairs,),
        args,
        specs,
        outs + [hot],
        [lead_block(o) for o in outs] + [whole(hot)],
        far_in=(0, 1, 2, 3, 4),
    )


def head_mask(h, width):
    lane = lax.broadcasted_iota(jnp.int32, (1, width), 1)
    return jnp.where((lane // HD) % 2 == h, 1.0, 0.0).astype(BF16)


def box_rows(tables, stream, head):
    row = tables[stream, pl.ds(head, 1), :]
    rolled = pltpu.roll(jnp.broadcast_to(row, (NBOX, PAIR)), NBOX, 1, stride=1, stride_axis=0)
    lane = lax.broadcasted_iota(jnp.int32, (NBOX, PAIR), 1)
    rolled = jnp.where(lane < NBOX, rolled, 0.0)
    high = rolled.astype(BF16)
    return jnp.concatenate([high, (rolled - high.astype(F32)).astype(BF16)], 0)


def rel_band(extended_row):
    wide = jnp.broadcast_to(extended_row, (BLK, 4 * BLK))
    return pltpu.roll(wide, 0, 1, stride=1, stride_axis=0)[:, BLK:]


def rel_bias(band, ends, block, blocks, skip):
    pieces = []
    for other in range(blocks):
        step = other - block
        if step >= 2:
            pieces.append(jnp.broadcast_to(ends[1], (ROWS, BLK)))
        elif step <= -2:
            pieces.append(jnp.broadcast_to(ends[0], (ROWS, BLK)))
        else:
            pieces.append(band[skip : skip + ROWS, (step + 1) * BLK : (step + 2) * BLK])
    return jnp.concatenate(pieces, 1)


def rel_parts(rel, head):
    row = rel[pl.ds(head, 1), :]
    ends = (row[:, :1], row[:, NREL - 1 :])
    low, high = (jnp.broadcast_to(e, (1, NREL // 2)) for e in ends)
    return rel_band(jnp.concatenate([low, row, high], 1)), ends


def accumulate(out, term):
    @pl.when(pl.program_id(0) == 0)
    def _():
        out[...] = term

    @pl.when(pl.program_id(0) > 0)
    def _():
        out[...] += term


def accumulate_halves(top, bottom, term):
    half = top.shape[0]
    accumulate(top, term[:half])
    accumulate(bottom, term[half:])


def attend(scores_of, count, probs_ref, values):
    logs = []
    for b in range(count // ROWS):
        scores = scores_of(b)
        peak = jnp.max(scores, 1, keepdims=True)
        powers = jnp.exp(scores - peak)
        total = jnp.sum(powers, 1, keepdims=True)
        probs_ref[b * ROWS : (b + 1) * ROWS, :] = (powers * (1.0 / total)).astype(BF16)
        logs.append(peak + jnp.log(total))
    return mm(probs_ref[...], values), jnp.concatenate(logs, 0)


def forward_body(
    vlen, tqs, vq, tks, tv, vk, vv, hot_q, hot, rel, tables, wo, attn, to, vo, lse, s_ref, p_ref, *, first
):
    count = tqs.shape[1]
    keys_n = tks.shape[1]
    keys_t = jnp.concatenate([tks[0], hot[0]], 1)
    keys_v = jnp.concatenate([vk[0], hot[1]], 1)
    valid = lax.broadcasted_iota(jnp.int32, (1, keys_n), 1) < vlen[0]
    lane = lax.broadcasted_iota(jnp.int32, (count, PAIR), 1)
    text_out, vis_out, logs = [], [], []
    for h in range(2):
        head = 2 * pl.program_id(0) + h
        look_t = mm_nt(hot_q[0], box_rows(tables, 0, head)).astype(BF16)
        look_v = mm_nt(hot_q[0], box_rows(tables, 1, head)).astype(BF16)
        query_t = jnp.concatenate([tqs[0] * head_mask(h, 2 * PAIR), look_t], 1)
        query_v = jnp.concatenate([vq[0] * head_mask(h, PAIR), look_v], 1)
        band, ends = rel_parts(rel, head)
        s_ref[2 * h] = mm_nt(query_t, keys_t)
        s_ref[2 * h + 1] = mm_nt(query_v, keys_v)

        def text_scores(b, h=h, band=band, ends=ends):
            at = first + b * ROWS
            bias = rel_bias(band, ends, at // BLK, keys_n // BLK, at % BLK)
            return s_ref[2 * h, b * ROWS : (b + 1) * ROWS, :] + bias

        def vis_scores(b, h=h):
            return jnp.where(valid, s_ref[2 * h + 1, b * ROWS : (b + 1) * ROWS, :], MASKED)

        out, log = attend(text_scores, count, p_ref.at[2 * h], tv[0])
        text_out.append(out)
        logs.append(log)
        out, log = attend(vis_scores, count, p_ref.at[2 * h + 1], vv[0])
        vis_out.append(out)
        logs.append(log)
    out_t = jnp.where(lane < HD, text_out[0], text_out[1]).astype(BF16)
    out_v = jnp.where(lane < HD, vis_out[0], vis_out[1]).astype(BF16)
    to[...] = out_t
    vo[...] = out_v
    kept = jnp.zeros((count, PAIR), F32)
    for spot, log in zip((0, 2, 1, 3), logs):
        kept = jnp.where(lane == spot, log, kept)
    lse[0] = kept
    term = mm(jnp.concatenate([out_t, out_v], 1), jnp.concatenate([wo[0], wo[1]], 0))

    accumulate(attn, term)


def forward_rows(first, count, proj, vlen, rel, tables, w_out, deps=(), into=None):
    tqs, tks, tv, vq, vk, vv, hot = proj
    pairs, n, _ = tqs.shape
    d = w_out.shape[2]
    spot = first // count

    def rows_of(x):
        return pl.BlockSpec((1, count, x.shape[2]), lambda p: (p, spot, 0))

    return call(
        partial(forward_body, first=first),
        f"A{spot}",
        (pairs,),
        (vlen, tqs, vq, tks, tv, vk, vv, hot, hot, rel, tables, w_out),
        [
            pl.BlockSpec(memory_space=pltpu.SMEM),
            rows_of(tqs),
            rows_of(vq),
            lead_block(tks),
            lead_block(tv),
            lead_block(vk),
            lead_block(vv),
            pl.BlockSpec((1, count, PAIR), lambda p: (0, spot, 0)),
            whole(hot),
            whole(rel),
            whole(tables),
            pl.BlockSpec((2, PAIR, d), lambda p: (0, p, 0)),
        ],
        [
            sds((count, d)),
            sds((n, pairs * PAIR), BF16),
            sds((n, pairs * PAIR), BF16),
            sds((pairs, n, PAIR)),
        ],
        [
            pl.BlockSpec((count, d), lambda p: (0, 0)),
            pl.BlockSpec((count, PAIR), lambda p: (spot, p)),
            pl.BlockSpec((count, PAIR), lambda p: (spot, p)),
            pl.BlockSpec((1, count, PAIR), lambda p: (p, spot, 0)),
        ],
        [pltpu.VMEM((4, count, n), F32), pltpu.VMEM((4, count, n), BF16)],
        deps=deps,
        aliases=None if into is None else {1: into[1], 2: into[2], 3: into[3]},
    )


def scores_gradient(probs, grad_probs):
    inner = jnp.sum(grad_probs * probs, 1, keepdims=True)
    return (probs * (grad_probs - inner)).astype(BF16)


def box_gradient(hot, spread, out):
    high = spread.astype(BF16)
    rest = (spread - high.astype(F32)).astype(BF16)
    table = (mm_tn(hot, high) + mm_tn(hot, rest))[:NBOX]
    lane = lax.broadcasted_iota(jnp.int32, (NBOX, PAIR), 1)
    for h in range(2):
        mine = table if h == 0 else pltpu.roll(table, NBOX, 1)
        mine = jnp.where(lane < NBOX, mine, 0.0)
        sheared = pltpu.roll(mine, 1, 1, stride=1, stride_axis=0)
        out[0, h : h + 1, :] = jnp.sum(sheared, 0, keepdims=True)


def shear_sum(band):
    width = band.shape[1]
    rows = BLK
    while rows > 8:
        rows //= 2
        band = band[:rows] + pltpu.roll(band[rows:], width - rows, 1)
    row = lax.broadcasted_iota(jnp.int32, band.shape, 0)
    for bit in (4, 2, 1):
        band = jnp.where((row // bit) % 2 == 1, pltpu.roll(band, width - bit, 1), band)
    return jnp.sum(band, 0, keepdims=True)


def visual_back_body(vlen, vq, vk, vv, dvo, lse, hot_q, hot, tables, *refs, last):
    if last:
        before, dxq, dxv, g_box, ds_ref, pb_ref, s_ref, dp_ref = refs
    else:
        dxq, partial_kv, g_box, ds_ref, pb_ref, s_ref, dp_ref = refs
    count = vq.shape[1]
    keys = jnp.concatenate([vk[0], hot[1]], 1)
    valid = lax.broadcasted_iota(jnp.int32, (1, vk.shape[1]), 1) < vlen[0]
    dq = dkt = dvt = spread = None
    for h in range(2):
        mask = head_mask(h, PAIR)
        look = mm_nt(hot_q[0], box_rows(tables, 1, 2 * pl.program_id(0) + h)).astype(BF16)
        mine = vq[0] * mask
        query = jnp.concatenate([mine, look], 1)
        grad = dvo[...] * mask
        s_ref[...] = mm_nt(query, keys)
        dp_ref[...] = mm_nt(grad, vv[0])
        for b in range(count // ROWS):
            part = slice(b * ROWS, (b + 1) * ROWS)
            scores = jnp.where(valid, s_ref[part, :], MASKED)
            probs = jnp.exp(scores - lse[0, part, 2 + h : 3 + h])
            pb_ref[part, :] = probs.astype(BF16)
            ds_ref[part, :] = scores_gradient(probs, dp_ref[part, :])
        ds, pb = ds_ref[...], pb_ref[...]
        terms = (mm(ds, vk[0] * mask), mm_tn(mine, ds), mm_tn(grad, pb), mm(ds, hot[3] * mask))
        if h == 0:
            dq, dkt, dvt, spread = terms
        else:
            dq, dkt, dvt, spread = (a + b for a, b in zip((dq, dkt, dvt, spread), terms))
    box_gradient(hot_q[0], spread, g_box)
    dxq[...] = (dq * SCALE).astype(BF16)
    if last:
        both = jnp.concatenate(
            [(before[0, :PAIR] + dkt).astype(BF16), (before[0, PAIR:] + dvt).astype(BF16)], 0
        ).T
        dxv[...] = both
    else:
        partial_kv[0, :PAIR] = dkt
        partial_kv[0, PAIR:] = dvt


def visual_back(spot, proj, vlen, tables, dvo, lse, before=None, deps=()):
    vq, vk, vv, hot = proj[3:]
    pairs, n, _ = vq.shape
    count = n // 2
    last = before is not None

    def rows_of(x):
        return pl.BlockSpec((1, count, x.shape[2]), lambda p: (p, spot, 0))

    half = pl.BlockSpec((count, PAIR), lambda p: (spot, p))
    args = (vlen, vq, vk, vv, dvo, lse, hot, hot, tables)
    specs = [
        pl.BlockSpec(memory_space=pltpu.SMEM),
        rows_of(vq),
        lead_block(vk),
        lead_block(vv),
        half,
        rows_of(lse),
        pl.BlockSpec((1, count, PAIR), lambda p: (0, spot, 0)),
        whole(hot),
        whole(tables),
    ]
    box = sds((pairs, 8, PAIR))
    kept = sds((pairs, 2 * PAIR, n))
    outs, out_specs = [sds((n, pairs * PAIR), BF16)], [half]
    if last:
        args += (before[1],)
        specs += [lead_block(kept)]
        outs += [sds((n, pairs * 2 * PAIR), BF16), box]
        out_specs += [pair_block(n, 2 * PAIR), lead_block(box)]
    else:
        outs += [kept, box]
        out_specs += [lead_block(kept), lead_block(box)]
    return call(
        partial(visual_back_body, last=last),
        f"V{spot}",
        (pairs,),
        args,
        specs,
        outs,
        out_specs,
        [pltpu.VMEM((count, n), BF16)] * 2 + [pltpu.VMEM((count, n), F32)] * 2,
        deps=deps,
        aliases={0: before[0]} if last else None,
    )


def text_back_body(
    tqs, tks, tv, dto, lse, hot, rel, tables, dxq, dxh, dxs, g_box, g_rel, ds_ref, pb_ref, s_ref, dp_ref, *, pair
):
    n = tqs.shape[1]
    keys = jnp.concatenate([tks[0], hot[0]], 1)
    dq = dkt = dvt = spread = None
    for h in range(2):
        mask, wide_mask = head_mask(h, PAIR), head_mask(h, 2 * PAIR)
        look = mm_nt(hot[0], box_rows(tables, 0, 2 * pair + h)).astype(BF16)
        mine = tqs[0] * wide_mask
        query = jnp.concatenate([mine, look], 1)
        grad = dto[...] * mask
        band, ends = rel_parts(rel, 2 * pair + h)
        near = [None] * 3
        low = high = jnp.zeros((BLK, BLK), F32)
        s_ref[...] = mm_nt(query, keys)
        dp_ref[...] = mm_nt(grad, tv[0])
        for b in range(n // ROWS):
            part = slice(b * ROWS, (b + 1) * ROWS)
            at = b * ROWS
            bias = rel_bias(band, ends, at // BLK, n // BLK, at % BLK)
            probs = jnp.exp(s_ref[part, :] + bias - lse[0, part, h : h + 1])
            pb_ref[part, :] = probs.astype(BF16)
            ds_ref[part, :] = scores_gradient(probs, dp_ref[part, :])
        for b in range(n // BLK):
            ds = ds_ref[b * BLK : (b + 1) * BLK, :].astype(F32)
            for other in range(n // BLK):
                piece = ds[:, other * BLK : (other + 1) * BLK]
                step = other - b
                if step >= 2:
                    high = high + piece
                elif step <= -2:
                    low = low + piece
                else:
                    near[step + 1] = piece if near[step + 1] is None else near[step + 1] + piece
        ds, pb = ds_ref[...], pb_ref[...]
        sums = shear_sum(jnp.concatenate(near + [jnp.zeros((BLK, BLK), F32)], 1))
        far = jnp.concatenate(
            [jnp.sum(low, 0, keepdims=True), jnp.sum(high, 0, keepdims=True)], 1
        )
        g_rel[0, 2 * h : 2 * h + 1, :] = sums
        g_rel[0, 2 * h + 1 : 2 * h + 2, : 2 * BLK] = far
        terms = (mm(ds, tks[0] * wide_mask), mm_tn(mine, ds), mm_tn(grad, pb), mm(ds, hot[2] * mask))
        if h == 0:
            dq, dkt, dvt, spread = terms
        else:
            dq, dkt, dvt, spread = (a + b for a, b in zip((dq, dkt, dvt, spread), terms))
    box_gradient(hot[0], spread, g_box)
    dqs = (dq * SCALE).astype(BF16)
    rest = jnp.concatenate([dkt.astype(BF16), dvt.astype(BF16)], 0).T
    dxs[...] = jnp.concatenate([dqs[:, PAIR:], rest[:, PAIR : 2 * PAIR]], 1)
    dxh[...] = jnp.concatenate([dqs[:, :PAIR], rest[:, :PAIR], rest[:, 2 * PAIR :], dxq[...]], 1)


def text_back(pair, proj, rel, tables, dto, lse, dxq, into=None, deps=()):
    tqs, tks, tv = proj[:3]
    hot = proj[6]
    pairs, n, _ = tqs.shape

    def lead(x):
        return pl.BlockSpec((1,) + x.shape[1:], lambda p: (pair, 0, 0))

    def block(width):
        return pl.BlockSpec((n, width), lambda p: (0, pair))

    outs = [
        sds((n, pairs * 4 * PAIR), BF16),
        sds((n, pairs * 2 * PAIR), BF16),
        sds((pairs, 8, PAIR)),
        sds((pairs, 8, 4 * BLK)),
    ]
    return call(
        partial(text_back_body, pair=pair),
        f"T{pair}",
        (1,),
        (tqs, tks, tv, dto, lse, hot, rel, tables, dxq),
        [lead(tqs), lead(tks), lead(tv), block(PAIR), lead(lse), whole(hot), whole(rel), whole(tables), block(PAIR)],
        outs,
        [block(4 * PAIR), block(2 * PAIR), lead(outs[2]), lead(outs[3])],
        [pltpu.VMEM((n, n), BF16)] * 2 + [pltpu.VMEM((n, n), F32)] * 2,
        deps=deps,
        aliases=None if into is None else {k: into[k] for k in range(4)},
    )


def spatial_part_body(dxs, wt, out):
    accumulate(out, mm_nt(dxs[...], jnp.concatenate([wt[3], wt[4]], 1)))


def spatial_part(dxs, w_text, deps=()):
    n, d = dxs.shape[0], w_text.shape[1]
    return call(
        spatial_part_body,
        "SP",
        (dxs.shape[1] // (2 * PAIR),),
        (dxs, w_text),
        [pair_block(n, 2 * PAIR), pl.BlockSpec((5, d, PAIR), lambda p: (0, 0, p))],
        sds((n, d)),
        pl.BlockSpec((n, d), lambda p: (0, 0)),
        deps=deps,
    )


def visual_part_body(dxv, wv, out):
    accumulate(out, mm_nt(dxv[...], jnp.concatenate([wv[1], wv[2]], 1)))


def visual_part(dxv, w_vis, deps=()):
    n, d = dxv.shape[0], w_vis.shape[1]
    return call(
        visual_part_body,
        "VP",
        (dxv.shape[1] // (2 * PAIR),),
        (dxv, w_vis),
        [pair_block(n, 2 * PAIR), pl.BlockSpec((3, d, PAIR), lambda p: (0, 0, p))],
        sds((n, d)),
        pl.BlockSpec((n, d), lambda p: (0, 0)),
        deps=deps,
    )


def hidden_part_body(dxh, wt, wv, out):
    accumulate(out, mm_nt(dxh[...], jnp.concatenate([wt[0], wt[1], wt[2], wv[0]], 1)))


def hidden_part(dxh, w_text, w_vis, deps=()):
    n, d = dxh.shape[0], w_text.shape[1]
    return call(
        hidden_part_body,
        "HP",
        (dxh.shape[1] // (4 * PAIR),),
        (dxh, w_text, w_vis),
        [
            pair_block(n, 4 * PAIR),
            pl.BlockSpec((5, d, PAIR), lambda p: (0, 0, p)),
            pl.BlockSpec((3, d, PAIR), lambda p: (0, 0, p)),
        ],
        sds((n, d)),
        pl.BlockSpec((n, d), lambda p: (0, 0)),
        deps=deps,
    )


def normalise(values):
    centred = values - jnp.mean(values, 1, keepdims=True)
    rstd = lax.rsqrt(jnp.mean(centred * centred, 1, keepdims=True) + EPSILON)
    return centred * rstd, rstd


def norm_back(grad, unit, rstd, gain):
    scaled = grad * gain
    mean_one = jnp.mean(scaled, 1, keepdims=True)
    mean_two = jnp.mean(scaled * unit, 1, keepdims=True)
    return rstd * (scaled - mean_one - unit * mean_two)


def column_sum(x):
    return jnp.sum(x, 0, keepdims=True)


def up_body(hid, own, got, gain, bias, w_up, b_up, w_down, h1b, z, r1, h1, slope, f):
    @pl.when(pl.program_id(0) == 0)
    def _():
        total = hid[...].astype(F32) + (own[...] + got[...])
        unit, _ = normalise(total)
        normed = unit * gain[0:1, :] + bias[0:1, :]
        r1[...] = total
        h1[...] = normed
        h1b[...] = normed.astype(BF16)

    u = mm(h1b[...], w_up[...]) + b_up[...]
    cdf = 0.5 * (1.0 + lax.erf(u * (0.5**0.5)))
    slope[...] = cdf + u * (jnp.exp(-0.5 * u * u) * 0.3989422804014327)
    active = (u * cdf).astype(BF16)
    z[...] = active
    accumulate(f, mm(active, w_down[...]))


def row_call(
    body, name, spot, grid, args, specs, outs, out_specs, halved, deps, into, far=(), far_in=()
):
    return call(
        body,
        f"{name}{spot}",
        grid,
        args,
        specs,
        outs,
        out_specs,
        deps=deps,
        aliases=None if into is None else {k: into[k] for k in halved},
        far=halved + far,
        far_in=far_in,
    )


def up_rows(spot, hidden, own, got, gain, bias, w_up, b_up, w_down, deps=(), into=None):
    n, d = hidden.shape
    ff = w_up.shape[1]
    count, block = n // 2, ff // FF_STEPS
    half = pl.BlockSpec((count, d), lambda p: (spot, 0))
    own_half = pl.BlockSpec((count, d), lambda p: (0, 0))
    args = (hidden, own, got, gain, bias, w_up, b_up, w_down)
    specs = [half, own_half, own_half, whole(gain), whole(bias), pair_block(d, block)]
    specs += [pair_block(1, block), pl.BlockSpec((block, d), lambda p: (p, 0))]
    outs = [sds((n, d), BF16), sds((n, ff), BF16), sds((count, d)), sds((count, d))]
    outs += [sds((count, ff)), sds((count, d))]
    out_specs = [half, pl.BlockSpec((count, block), lambda p: (spot, p)), own_half, own_half]
    out_specs += [pair_block(count, block), own_half]
    return row_call(
        up_body, "F", spot, (FF_STEPS,), args, specs, outs, out_specs, (0, 1), deps, into, (4,), (0, 5, 7)
    )


def down_body(
    h1, own, got, cot, gain, bias, b_down, w_down, w_up, slope, result, df, du, dr2, pd, sums, sum_up
):
    @pl.when(pl.program_id(0) == 0)
    def _():
        total = h1[...] + ((own[...] + got[...]) + b_down[...])
        unit, rstd = normalise(total)
        result[...] = (unit * gain[1:2, :] + bias[1:2, :]).astype(BF16)
        grad = cot[...].astype(F32)
        back = norm_back(grad, unit, rstd, gain[1:2, :])
        low = back.astype(BF16)
        dr2[...] = back
        df[...] = low
        sums[0:1, :] = column_sum(grad * unit)
        sums[1:2, :] = column_sum(grad)
        sums[2:3, :] = column_sum(low.astype(F32))

    grad_u = (slope[...] * mm_nt(df[...], w_down[...])).astype(BF16)
    du[...] = grad_u
    sum_up[0:1, :] = column_sum(grad_u.astype(F32))
    accumulate(pd, mm_nt(grad_u, w_up[...]))


def down_rows(spot, h1, own, got, cotangent, gain, bias, b_down, w_down, w_up, slope, deps=(), into=None):
    n, d = cotangent.shape
    ff = w_up.shape[1]
    count, block = n // 2, ff // FF_STEPS
    half = pl.BlockSpec((count, d), lambda p: (spot, 0))
    own_half = pl.BlockSpec((count, d), lambda p: (0, 0))
    args = (h1, own, got, cotangent, gain, bias, b_down, w_down, w_up, slope)
    specs = [own_half] * 3 + [half, whole(gain), whole(bias), whole(b_down)]
    specs += [pl.BlockSpec((block, d), lambda p: (p, 0)), pair_block(d, block), pair_block(count, block)]
    outs = [sds((n, d), BF16), sds((n, d), BF16), sds((n, ff), BF16), sds((count, d))]
    outs += [sds((count, d)), sds((8, d)), sds((8, ff))]
    out_specs = [half, half, pl.BlockSpec((count, block), lambda p: (spot, p)), own_half, own_half]
    out_specs += [whole(outs[5]), pair_block(8, block)]
    return row_call(
        down_body,
        "B",
        spot,
        (FF_STEPS,),
        args,
        specs,
        outs,
        out_specs,
        (0, 1, 2),
        deps,
        into,
        far_in=(3, 7, 8, 9),
    )


def first_body(dr2, own, got, r1, gain, w_out, dr1, da, dto, dvo, sums):
    grad = dr2[...] + (own[...] + got[...])
    unit, rstd = normalise(r1[...])
    back = norm_back(grad, unit, rstd, gain[0:1, :])
    low = back.astype(BF16)
    dr1[...] = back
    da[...] = low
    dto[...] = mm_nt(low, w_out[0]).astype(BF16)
    dvo[...] = mm_nt(low, w_out[1]).astype(BF16)
    sums[0:1, :] = column_sum(grad * unit)
    sums[1:2, :] = column_sum(grad)


def first_rows(spot, dr2, own, got, r1, gain, w_out, deps=(), into=None):
    n, d = 2 * own.shape[0], own.shape[1]
    width = w_out.shape[1]
    args = (dr2, own, got, r1, gain, w_out)
    outs = [sds((n, d)), sds((n, d), BF16)]
    outs += [sds((n, width), BF16), sds((n, width), BF16), sds((8, d))]
    out_specs = [pl.BlockSpec((n // 2, x.shape[1]), lambda p: (spot, 0)) for x in outs[:4]] + [whole(outs[4])]
    return row_call(
        first_body,
        "N",
        spot,
        (1,),
        args,
        [whole(x) for x in args],
        outs,
        out_specs,
        (0, 1, 2, 3),
        deps,
        into,
    )


def pack_body(one_a, one_b, two_a, two_b, up_a, up_b, g_rel, g_box_t, g_box_v, g_box_w, out):
    d = out.shape[1]
    one = one_a[...] + one_b[...]
    two = two_a[...] + two_b[...]
    up = up_a[...] + up_b[...]
    out[...] = jnp.zeros(out.shape, F32)
    out[0:1, :] = one[0:1]
    out[1:2, :] = two[0:1]
    out[2:3, :] = one[1:2]
    out[3:4, :] = two[1:2]
    out[4:5, :] = two[2:3]
    out[5:6, :] = up[0:1, :d]
    out[6:7, :] = up[0:1, d:]
    half = NREL // 2
    lane = lax.broadcasted_iota(jnp.int32, (1, 2 * NREL), 1)
    for head in range(2 * g_rel.shape[0]):
        p, h = head // 2, head % 2
        near = g_rel[p, 2 * h : 2 * h + 1, :]
        far = g_rel[p, 2 * h + 1 : 2 * h + 2, :NREL]
        low = jnp.sum(jnp.where((lane > 3 * half) | (lane == 0), near, 0.0), 1, keepdims=True)
        low = low + jnp.sum(far[:, :half], 1, keepdims=True)
        high = jnp.sum(jnp.where((lane >= 2 * half - 1) & (lane < 3 * half), near, 0.0), 1, keepdims=True)
        high = high + jnp.sum(far[:, half:], 1, keepdims=True)
        short = lane[:, :NREL]
        row = jnp.where(short == 0, low, jnp.where(short == NREL - 1, high, near[:, :NREL]))
        spot = 8 + head
        out[spot : spot + 1, :NREL] = row
        out[spot : spot + 1, NREL : NREL + PAIR] = g_box_t[p, h : h + 1, :]
        out[spot : spot + 1, NREL + PAIR : NREL + 2 * PAIR] = (
            g_box_v[p, h : h + 1, :] + g_box_w[p, h : h + 1, :]
        )


def pack_small(d, args, deps=()):
    heads = 2 * args[6].shape[0]
    out = sds((8 + -(-heads // 8) * 8, d))
    return call(
        pack_body, "SK", (1,), args, [whole(x) for x in args], out, whole(out), deps=deps
    )


def unpack_body(own, rel, space, gain, bias, b_up, b_down):
    x = own[...]
    d = x.shape[1]
    gain[...] = x[0:2]
    bias[...] = x[2:4]
    b_down[...] = x[4:5]
    b_up[:, :d] = x[5:6]
    b_up[:, d:] = x[6:7]
    heads = rel.shape[0]
    rel[...] = x[8 : 8 + heads, :NREL]
    space[0] = x[8 : 8 + heads, NREL : NREL + PAIR]
    space[1] = x[8 : 8 + heads, NREL + PAIR : NREL + 2 * PAIR]


def unpack_small(own, heads, ff, deps=()):
    d = own.shape[1]
    outs = [sds((heads, NREL)), sds((2, heads, PAIR)), sds((2, d)), sds((2, d)), sds((1, ff)), sds((1, d))]
    return call(
        unpack_body, "SU", (1,), (own,), [whole(own)], outs, [whole(x) for x in outs], deps=deps
    )


def place_rows(order, left, plain, placed, chunk):
    if chunk is None:
        placed[...] = left[...].T
    else:
        plain[...] = left[...].T
        for r in range(plain.shape[0] // chunk):
            spot = pl.multiple_of(order[r] * chunk, chunk)
            placed[r * chunk : (r + 1) * chunk, :] = plain[pl.ds(spot, chunk), :]


def product_body(order, *refs, sets, chunk):
    count = sum(1 + cols for cols in sets)
    ins, mine = refs[:count], refs[count]
    others, scratch = refs[count + 1 : -2 * len(sets)], refs[-2 * len(sets) :]
    half = mine.shape[0]
    p = pl.program_id(0)
    at = column = 0
    for k, cols in enumerate(sets):
        left, right = ins[at], [c[...] for c in ins[at + 1 : at + 1 + cols]]
        plain, placed = scratch[2 * k : 2 * k + 2]
        at += 1 + cols
        if len(sets) > 1:
            place_rows(order, left, plain, placed, chunk)
        else:

            @pl.when(p == 0)
            def _():
                place_rows(order, left, plain, placed, chunk)

        out = mm(placed[...], right[0] if cols == 1 else jnp.concatenate(right, 1))
        mine[:, column : column + out.shape[1]] = out[:half]
        column += out.shape[1]
        if not others:
            pass
        elif len(sets) > 1:
            others[k][...] = out[half:]
        else:
            for step, other in enumerate(others):

                @pl.when(p == step)
                def _(other=other, out=out):
                    other[...] = out[half:]


def weight_product(name, links, way, sets, steps=1, deps=(), together=False):
    n, d = sets[0][0].shape
    chunk = d // links.n
    order = links.order(way, together)
    args, specs = [order], [pl.BlockSpec(memory_space=pltpu.SMEM)]
    for rows, cols in sets:
        if chunk % 16:
            rows = jnp.take(rows.reshape(n, links.n, chunk), order, axis=1, mode="clip").reshape(n, d)
        args += [rows, *cols]
        specs += [whole(rows)] + [pair_block(n, c.shape[1] // steps) for c in cols]
    widths = [sum(c.shape[1] for c in cols) // steps for _, cols in sets]
    height = d if together else d // 2
    blocks = [] if together else widths * steps
    return call(
        partial(product_body, sets=[len(cols) for _, cols in sets], chunk=None if chunk % 16 else chunk),
        name,
        (steps,),
        tuple(args),
        specs,
        [sds((height, steps * sum(widths)))] + [sds((d // 2, w)) for w in blocks],
        [pair_block(height, sum(widths))] + [pl.BlockSpec((d // 2, w), lambda p: (0, 0)) for w in blocks],
        [pltpu.VMEM((d, n), BF16)] * (2 * len(sets)),
        deps=deps,
    )


def flat(terms):
    return [x for arrays, _ in terms for x in arrays]


def sum_terms(refs, counts):
    total, at = None, 0
    for count in counts:
        pieces = [ref[...] for ref in refs[at : at + count]]
        at += count
        value = pieces[0] if count == 1 else jnp.concatenate(pieces, 1)
        total = value if total is None else total + value
    return total


def add_body(*refs, counts):
    refs[-1][...] = sum_terms(refs[:-1], counts)


def add_chunks(name, terms, rows, first, blocks, deps=()):
    width = sum(x.shape[1] for x in terms[0][0])
    if rows % 8:
        values = [
            jnp.concatenate([x[(at + first) * rows : (at + first + blocks) * rows] for x in arrays], 1)
            for arrays, at in terms
        ]
        return sum(values[1:], values[0])
    step = max(1, blocks // 2)
    args = flat(terms)
    return call(
        partial(add_body, counts=[len(arrays) for arrays, _ in terms]),
        name,
        (blocks // step,),
        tuple(args),
        [
            pl.BlockSpec((step * rows, x.shape[1]), lambda p, at=at: ((at + first) // step + p, 0))
            for arrays, at in terms
            for x in arrays
        ],
        sds((blocks * rows, width)),
        pl.BlockSpec((step * rows, width), lambda p: (p, 0)),
        deps=deps,
    )


def total_body(*refs):
    *first, own, got, out = refs
    total = own[...] + got[...]
    for ref in first:
        total = ref[...] + total
    out[...] = total.astype(out.dtype)


def total_rows(name, spot, own, got, dtype, first=(), deps=(), into=None, parts=2):
    count, d = own.shape
    steps = 4 // parts
    block = pl.BlockSpec((count // steps, d), lambda p: (p, 0))
    placed = pl.BlockSpec((count // steps, d), lambda p: (steps * spot + p, 0))
    return call(
        total_body,
        f"{name}{spot}",
        (steps,),
        (*first, own, got),
        [placed] * len(first) + [block, block],
        sds((parts * count, d), dtype),
        placed,
        deps=deps,
        aliases=None if into is None else {0: into},
    )


def add_small(x, y, deps=()):
    return call(
        partial(add_body, counts=[1, 1]), "SS", (1,), (x, y), [whole(x)] * 2, sds(x.shape), whole(x), deps=deps
    )


class Links:
    def __init__(self, sizes):
        self.n = sizes["dp"]
        bits = [1 << k for k in range(self.n.bit_length() - 1)]
        core, side, *ring = bits
        self.side_first = [core, side, *ring]
        self.ring_first = [core, *ring[:1], side, *ring[1:]]

    def order(self, way, together=False):
        flips = []
        for p in range(self.n):
            flips.append(sum(bit for k, bit in enumerate(way) if p >> (len(way) - 1 - k) & 1))
        me = lax.axis_index("dp")
        return jnp.array(flips, jnp.int32) ^ (me - me % 2 if together else me)

    def cores(self, x):
        groups = [[d, d + 1] for d in range(0, self.n, 2)]
        return lax.all_to_all(x, "dp", 0, 0, axis_index_groups=groups, tiled=True)

    def across(self, x):
        return lax.ppermute(x, "tensor", [(0, 1), (1, 0)])

    def swap(self, x, bit):
        return lax.ppermute(x, "dp", [(d, d ^ bit) for d in range(self.n)])


class Scatter:
    def __init__(self, name, links, way, halves):
        self.name, self.links, self.left = name, links, list(way)
        mine, *others = halves
        self.blocks = links.n // 2
        first = self.left.pop(0)
        if others:
            self.rows = 2 * mine.shape[0] // links.n
            self.terms = [((mine,), 0), (tuple(links.swap(other, first) for other in others), 0)]
        else:
            self.rows = mine.shape[0] // links.n
            both = links.cores(mine)
            self.terms = [((both,), 0), ((both,), self.blocks)]

    def step(self, deps=()):
        if not self.left:
            return deps[0]
        self.blocks //= 2
        name = f"{self.name}{len(self.terms) - 2}"
        out = add_chunks(name, self.terms, self.rows, self.blocks, self.blocks, deps)
        self.terms.append(((self.links.swap(out, self.left.pop(0)),), 0))
        return out

    def rest(self, deps=()):
        while self.left:
            deps = (self.step(deps),)
        return deps

    def total(self, deps=()):
        deps = self.rest(deps)
        return add_chunks(f"{self.name}T", self.terms, self.rows, 0, 1, deps)


def spread_body(*refs, counts, places, ready):
    groups = [sum(c) for c in counts]
    ins, out_refs = refs[: sum(groups)], refs[sum(groups) + len(ready) :]
    for ref, (out, m) in zip(refs[sum(groups) :], ready):
        out_refs[out][m : m + ref.shape[0]] = ref[...]
    at = 0
    for count, place in zip(counts, places):
        total = sum_terms(ins[at : at + sum(count)], count)
        at += sum(count)
        for k, (out, m, p) in enumerate(place):
            out_refs[out][m, :, p * PAIR : (p + 1) * PAIR] = total[:, k * PAIR : (k + 1) * PAIR]


def spread(name, scatters, places, outs, deps=(), ready=()):
    rows = scatters[0].rows
    for s in scatters:
        deps = s.rest(deps)
    if rows % 8:
        parts = {}
        for s, place in zip(scatters, places):
            total = s.total(deps)
            for k, key in enumerate(place):
                parts[key] = total[:, k * PAIR : (k + 1) * PAIR]
        for x, out, first in ready:
            for m in range(x.shape[0]):
                for p in range(x.shape[2] // PAIR):
                    parts[out, first + m, p] = x[m, :, p * PAIR : (p + 1) * PAIR]
        return [
            jnp.stack(
                [
                    jnp.concatenate([parts[o, m, p] for p in range(x.shape[2] // PAIR)], 1)
                    for m in range(x.shape[0])
                ]
            )
            for o, x in enumerate(outs)
        ]
    args = [x for s in scatters for x in flat(s.terms)]
    return call(
        partial(
            spread_body,
            counts=[[len(t) for t, _ in s.terms] for s in scatters],
            places=places,
            ready=[(out, first) for _, out, first in ready],
        ),
        name,
        (1,),
        (*args, *(x for x, _, _ in ready)),
        [
            pl.BlockSpec((rows, x.shape[1]), lambda p, at=at: (at, 0))
            for s in scatters
            for arrays, at in s.terms
            for x in arrays
        ]
        + [whole(x) for x, _, _ in ready],
        outs,
        [whole(x) for x in outs],
        deps=deps,
    )


def on_device(
    links,
    hidden,
    spatial,
    visual,
    vis_len,
    text_box,
    vis_box,
    text_weight_matrix,
    w_vis,
    w_out,
    rel_table,
    space_tables,
    norm_gain,
    norm_bias,
    w_up,
    b_up,
    w_down,
    b_down,
    cotangent,
):
    Plan.begin()
    n, d = hidden.shape
    width = w_vis.shape[2]
    pairs = width // PAIR
    ff = w_up.shape[1]
    heads = rel_table.shape[0]
    text_row, vis_row = text_box.reshape(1, n), vis_box.reshape(1, -1)
    b_up_row, b_down_row = b_up.reshape(1, ff), b_down.reshape(1, d)

    proj = projections(hidden, spatial, visual, text_weight_matrix, w_vis, text_row, vis_row)
    count = n // 2
    common = (proj, vis_len, rel_table, space_tables, w_out)
    front_a = forward_rows(0, count, *common)
    got_a = links.across(front_a[0])
    front_b = forward_rows(count, count, *common, deps=(front_a[0],), into=front_a)
    got_b = links.across(front_b[0])
    merged_t, merged_v, lse = front_b[1:]

    feed = (norm_gain, norm_bias, w_up, b_up_row, w_down)
    up_a = up_rows(0, hidden, front_a[0], got_a, *feed, deps=(front_b[0],))
    got_a = links.across(up_a[5])
    up_b = up_rows(1, hidden, front_b[0], got_b, *feed, deps=(up_a[5],), into=up_a)
    got_b = links.across(up_b[5])
    h1_low, active = up_b[:2]

    feed = (cotangent, norm_gain, norm_bias, b_down_row, w_down, w_up)
    down_a = down_rows(0, up_a[3], up_a[5], got_a, *feed, up_a[4], deps=(up_b[5],))
    got_a = links.across(down_a[4])
    down_b = down_rows(1, up_b[3], up_b[5], got_b, *feed, up_b[4], deps=(down_a[4],), into=down_a)
    got_b = links.across(down_b[4])
    result, df, du = down_b[:3]

    way_a, way_b = links.side_first, links.ring_first
    half_down = weight_product("pD", links, way_a, [(df, (active,))], 2, (down_b[4],))
    sc_down = Scatter("D", links, way_a, half_down)
    half_up = weight_product("pU", links, way_b, [(h1_low, (du,))], 2, half_down[:1])
    sc_up = Scatter("U", links, way_b, half_up)
    first_a = first_rows(
        0, down_a[3], down_a[4], got_a, up_a[2], norm_gain, w_out, deps=half_up[:1]
    )
    last = sc_down.step((first_a[4],))
    last = sc_up.step((last,))
    vis_a = visual_back(0, proj, vis_len, space_tables, first_a[3], lse, deps=(last,))
    first_b = first_rows(
        1, down_b[3], down_b[4], got_b, up_b[2], norm_gain, w_out, deps=vis_a[1:2], into=first_a
    )
    dr1, da, dto, dvo = first_b[:4]
    dxq, dxv, g_box_vis = visual_back(
        1, proj, vis_len, space_tables, dvo, lse, before=vis_a, deps=(first_b[4],)
    )
    half_mixed = weight_product(
        "pM",
        links,
        way_a,
        [(da, (merged_t, merged_v)), (visual, (dxv,))],
        1,
        (g_box_vis,),
    )
    sc_mixed = Scatter("M", links, way_a, half_mixed)
    part_vis = visual_part(dxv, w_vis, half_mixed[:1])
    got_vis = links.across(part_vis)
    last = sc_down.step((part_vis,))
    last = sc_up.step((last,))
    text = text_back(0, proj, rel_table, space_tables, dto, lse, dxq, None, (last,))
    last = sc_mixed.step((text[2],))
    text = text_back(1, proj, rel_table, space_tables, dto, lse, dxq, text, (last,))
    dxh, dxs, g_box_text, g_rel = text_back(
        2, proj, rel_table, space_tables, dto, lse, dxq, text, text[2:3]
    )
    last = small = pack_small(
        d,
        (first_a[4], first_b[4], down_a[5], down_b[5], down_a[6], down_b[6])
        + (g_rel, g_box_text, vis_a[2], g_box_vis),
    )
    bits = list(links.side_first)

    def small_step(x, deps):
        return add_small(x, links.swap(x, bits.pop(0)), deps)

    part_spa = spatial_part(dxs, text_weight_matrix, (last,))
    got_spa = links.across(part_spa)
    last = sc_up.step((part_spa,))
    last = sc_down.step((last,))
    half_hid = weight_product(
        "pH", links, way_a, [(hidden, (dxh,))], 2, (last,), together=True
    )
    sc_hid = Scatter("H", links, way_a, half_hid)
    last = sc_hid.step(half_hid[:1])
    last = grad_visual = total_rows("VT", 0, part_vis, got_vis, F32, deps=(last,), parts=1)
    last = sc_mixed.step((last,))
    last = g_w_up = sc_up.total((last,))
    half_spa = weight_product(
        "pS", links, way_b, [(spatial, (dxs,))], 1, (last,), together=True
    )
    sc_spa = Scatter("S", links, way_b, half_spa)
    last = sc_spa.step(half_spa[:1])
    last = g_w_down = sc_down.total((last,))
    part_hid = hidden_part(dxh, text_weight_matrix, w_vis, (last,))
    got_hid = links.across(part_hid)
    last = sc_mixed.step((part_hid,))
    last = sc_hid.step((last,))
    last = sc_spa.step((last,))
    last = grad_spatial = total_rows("ST", 0, part_spa, got_spa, F32, deps=(last,), parts=1)
    last = small = small_step(small, (last,))
    last = small = small_step(small, (last,))
    rows = d // links.n
    three = range(pairs)
    g_w_out, g_vis = spread(
        "MT",
        [sc_mixed],
        [[(0, m, p) for m in range(2) for p in three] + [(1, m, p) for p in three for m in range(2)]],
        [sds((2, rows, width))] * 2,
        (last,),
    )
    last = sc_spa.step((g_vis,))
    last = sc_hid.step((last,))
    while bits:
        last = small = small_step(small, (last,))
    last, *_ = g_rel_table, g_space, g_gain, g_bias, g_b_up, g_b_down = unpack_small(
        small, rel_table.shape[0], ff, (last,)
    )
    last = grad_hidden = total_rows("HT", 0, part_hid, got_hid, BF16, (dr1,), deps=(last,), parts=1)
    g_w_text, g_w_vis = spread(
        "AT",
        [sc_hid, sc_spa],
        [
            [((0, m, p) if m < 3 else (1, 0, p)) for p in three for m in range(4)],
            [(0, 3 + m, p) for p in three for m in range(2)],
        ],
        [sds((5, rows, width)), sds((3, rows, width))],
        (last,),
        [(g_vis, 1, 1)],
    )
    return (
        result,
        grad_hidden,
        grad_spatial,
        grad_visual,
        g_w_text,
        g_w_vis,
        g_w_out.transpose(0, 2, 1),
        g_rel_table,
        g_space,
        g_gain,
        g_bias,
        g_w_up,
        g_b_up.reshape(ff),
        g_w_down.T,
        g_b_down.reshape(d),
    )


def solution(mesh):
    return jax.shard_map(
        partial(on_device, Links(dict(mesh.shape))),
        mesh=mesh,
        in_specs=(
            P("dp", None),
            P("dp", None),
            P("dp", None),
            P("dp"),
            P("dp"),
            P("dp"),
            P(None, None, "tensor"),
            P(None, None, "tensor"),
            P(None, "tensor", None),
            P("tensor", None),
            P(None, "tensor", None),
            P(),
            P(),
            P(None, "tensor"),
            P("tensor"),
            P("tensor", None),
            P(),
            P("dp", None),
        ),
        out_specs=(
            P("dp", None),
            P("dp", None),
            P("dp", None),
            P("dp", None),
            P(None, "dp", "tensor"),
            P(None, "dp", "tensor"),
            P(None, "tensor", "dp"),
            P("tensor", None),
            P(None, "tensor", None),
            P(),
            P(),
            P("dp", "tensor"),
            P("tensor"),
            P("tensor", "dp"),
            P(),
        ),
        check_vma=False,
    )
```

```python
from functools import partial

import jax
import jax.numpy as jnp
from jax import lax
from jax.experimental import pallas as pl
from jax.experimental.pallas import tpu as pltpu
from jax.sharding import PartitionSpec as P

HD = 64
PAIR = 2 * HD
TEXT = 512
NREL = 256
NBOX = 64
BLK = 128
ROWS = 64
EPSILON = 1e-05
MASKED = -1e30
SCALE = HD ** (-0.5)
F32 = jnp.float32
BF16 = jnp.bfloat16
MIB = 1 << 20
VMEM = 18
COST = 0.35e9
FF_STEPS = 3


def mm(a, b):
    return jnp.dot(a, b, preferred_element_type=F32)


def mm_nt(a, b):
    return lax.dot_general(a, b, (((1,), (1,)), ((), ())), preferred_element_type=F32)


def mm_tn(a, b):
    return lax.dot_general(a, b, (((0,), (0,)), ((), ())), preferred_element_type=F32)


STARTS = (
    0.0, 4.0, 10.0, 36.0, 53.0, 70.0, 87.0, 95.0, 98.5, 104.5, 118.5, 119.5,
    120.5, 126.5, 128.0, 131.0, 134.0, 137.0, 138.5, 140.0, 144.0, 146.0, 150.0, 154.0,
    155.5, 158.0, 159.5, 161.0, 171.5, 173.5, 178.0, 179.5, 181.0, 188.5, 192.0, 194.0,
    198.0, 205.0, 207.0, 209.0, 210.0, 211.0, 213.0, 215.0, 222.0, 228.5, 231.5, 232.0,
    232.5, 233.0,
)


class Plan:
    left = []

    @classmethod
    def begin(cls):
        cls.left = [b - a for a, b in zip(STARTS, STARTS[1:])]

    @classmethod
    def weight(cls):
        return cls.left.pop(0) if cls.left else 1.0


def call(body, name, grid, args, in_specs, outs, out_specs, scratch=(), deps=(), aliases=None, far=(), far_in=()):
    aliases = dict(aliases or {})
    if far:
        outs = [pltpu.HBM(o.shape, o.dtype) if k in far else o for k, o in enumerate(outs)]
    args = [pltpu.with_memory_space_constraint(x, pltpu.HBM) if k in far_in else x for k, x in enumerate(args)]
    n_in, extra = len(args), list(aliases.values()) + list(deps)

    def inner(*refs):
        body(*refs[:n_in], *refs[n_in + len(extra) :])

    return pl.pallas_call(
        inner,
        out_shape=outs,
        grid_spec=pltpu.PrefetchScalarGridSpec(
            num_scalar_prefetch=0,
            grid=grid,
            in_specs=list(in_specs) + [pl.BlockSpec(memory_space=pl.ANY)] * len(extra),
            out_specs=out_specs,
            scratch_shapes=list(scratch),
        ),
        input_output_aliases={n_in + k: out for k, out in enumerate(aliases)},
        compiler_params=pltpu.CompilerParams(
            dimension_semantics=("arbitrary",) * len(grid), vmem_limit_bytes=VMEM * MIB
        ),
        cost_estimate=pl.CostEstimate(flops=int(COST * Plan.weight()), bytes_accessed=1000, transcendentals=0),
        name=name,
    )(*args, *extra)


def whole(x):
    nd = x.ndim
    return pl.BlockSpec(x.shape, lambda p: (0,) * nd)


def sds(shape, dtype=F32):
    return jax.ShapeDtypeStruct(shape, dtype)


def pair_block(rows, width):
    return pl.BlockSpec((rows, width), lambda p: (0, p))


def lead_block(x):
    nd = x.ndim
    return pl.BlockSpec((1,) + x.shape[1:], lambda p: (p,) + (0,) * (nd - 1))


def proj_body(hid, spa, vis, wt, wv, tb, vb, tqs, tks, tv, vq, vk, vv, hot):
    ph = mm(hid[...], jnp.concatenate([wt[0], wt[1], wt[2], wv[0]], 1)).astype(BF16)
    ps = mm(spa[...], jnp.concatenate([wt[3], wt[4]], 1)).astype(BF16)
    pv = mm(vis[...], jnp.concatenate([wv[1], wv[2]], 1)).astype(BF16)
    scale = jnp.asarray(SCALE, BF16)
    tqs[0, :, :PAIR] = ph[:, :PAIR] * scale
    tqs[0, :, PAIR:] = ps[:, :PAIR] * scale
    tks[0, :, :PAIR] = ph[:, PAIR : 2 * PAIR]
    tks[0, :, PAIR:] = ps[:, PAIR:]
    tv[0] = ph[:, 2 * PAIR : 3 * PAIR]
    vq[0] = ph[:, 3 * PAIR :] * scale
    vk[0] = pv[:, :PAIR]
    vv[0] = pv[:, PAIR:]

    @pl.when(pl.program_id(0) == 0)
    def _():
        row = lax.broadcasted_iota(jnp.int32, (PAIR, hot.shape[1]), 0) % HD
        for k, box in enumerate((tb, vb)):
            hot[k] = jnp.where(row == box[...], 1.0, 0.0).T.astype(BF16)
            hot[k + 2] = jnp.where(row == NBOX - 1 - box[...], 1.0, 0.0).T.astype(BF16)


def projections(hidden, spatial, visual, w_text, w_vis, text_box, vis_box):
    n, d = hidden.shape
    pairs = w_text.shape[2] // PAIR
    wide, slim = sds((pairs, n, 2 * PAIR), BF16), sds((pairs, n, PAIR), BF16)
    outs = [wide, wide, slim, slim, slim, slim]
    hot = sds((4, n, PAIR), BF16)
    args = (hidden, spatial, visual, w_text, w_vis, text_box, vis_box)
    specs = [whole(x) for x in args]
    specs[3] = pl.BlockSpec((5, d, PAIR), lambda p: (0, 0, p))
    specs[4] = pl.BlockSpec((3, d, PAIR), lambda p: (0, 0, p))
    return call(
        proj_body,
        "P",
        (pairs,),
        args,
        specs,
        outs + [hot],
        [lead_block(o) for o in outs] + [whole(hot)],
        far_in=(0, 1, 2, 3, 4),
    )


def head_mask(h, width):
    lane = lax.broadcasted_iota(jnp.int32, (1, width), 1)
    return jnp.where((lane // HD) % 2 == h, 1.0, 0.0).astype(BF16)


def box_rows(tables, stream, head):
    row = tables[stream, pl.ds(head, 1), :]
    rolled = pltpu.roll(jnp.broadcast_to(row, (NBOX, PAIR)), NBOX, 1, stride=1, stride_axis=0)
    lane = lax.broadcasted_iota(jnp.int32, (NBOX, PAIR), 1)
    rolled = jnp.where(lane < NBOX, rolled, 0.0)
    high = rolled.astype(BF16)
    return jnp.concatenate([high, (rolled - high.astype(F32)).astype(BF16)], 0)


def rel_band(extended_row):
    wide = jnp.broadcast_to(extended_row, (BLK, 4 * BLK))
    return pltpu.roll(wide, 0, 1, stride=1, stride_axis=0)[:, BLK:]


def rel_bias(band, ends, block, blocks, skip):
    pieces = []
    for other in range(blocks):
        step = other - block
        if step >= 2:
            pieces.append(jnp.broadcast_to(ends[1], (ROWS, BLK)))
        elif step <= -2:
            pieces.append(jnp.broadcast_to(ends[0], (ROWS, BLK)))
        else:
            pieces.append(band[skip : skip + ROWS, (step + 1) * BLK : (step + 2) * BLK])
    return jnp.concatenate(pieces, 1)


def rel_parts(rel, head):
    row = rel[pl.ds(head, 1), :]
    ends = (row[:, :1], row[:, NREL - 1 :])
    low, high = (jnp.broadcast_to(e, (1, NREL // 2)) for e in ends)
    return rel_band(jnp.concatenate([low, row, high], 1)), ends


def accumulate(out, term):
    @pl.when(pl.program_id(0) == 0)
    def _():
        out[...] = term

    @pl.when(pl.program_id(0) > 0)
    def _():
        out[...] += term


def accumulate_halves(top, bottom, term):
    half = top.shape[0]
    accumulate(top, term[:half])
    accumulate(bottom, term[half:])


def attend(scores_of, count, probs_ref, values):
    logs = []
    for b in range(count // ROWS):
        scores = scores_of(b)
        peak = jnp.max(scores, 1, keepdims=True)
        powers = jnp.exp(scores - peak)
        total = jnp.sum(powers, 1, keepdims=True)
        probs_ref[b * ROWS : (b + 1) * ROWS, :] = (powers * (1.0 / total)).astype(BF16)
        logs.append(peak + jnp.log(total))
    return mm(probs_ref[...], values), jnp.concatenate(logs, 0)


def forward_body(
    vlen, tqs, vq, tks, tv, vk, vv, hot_q, hot, rel, tables, wo, attn, to, vo, lse, s_ref, p_ref, *, first
):
    count = tqs.shape[1]
    keys_n = tks.shape[1]
    keys_t = jnp.concatenate([tks[0], hot[0]], 1)
    keys_v = jnp.concatenate([vk[0], hot[1]], 1)
    valid = lax.broadcasted_iota(jnp.int32, (1, keys_n), 1) < vlen[0]
    lane = lax.broadcasted_iota(jnp.int32, (count, PAIR), 1)
    text_out, vis_out, logs = [], [], []
    for h in range(2):
        head = 2 * pl.program_id(0) + h
        look_t = mm_nt(hot_q[0], box_rows(tables, 0, head)).astype(BF16)
        look_v = mm_nt(hot_q[0], box_rows(tables, 1, head)).astype(BF16)
        query_t = jnp.concatenate([tqs[0] * head_mask(h, 2 * PAIR), look_t], 1)
        query_v = jnp.concatenate([vq[0] * head_mask(h, PAIR), look_v], 1)
        band, ends = rel_parts(rel, head)
        s_ref[2 * h] = mm_nt(query_t, keys_t)
        s_ref[2 * h + 1] = mm_nt(query_v, keys_v)

        def text_scores(b, h=h, band=band, ends=ends):
            at = first + b * ROWS
            bias = rel_bias(band, ends, at // BLK, keys_n // BLK, at % BLK)
            return s_ref[2 * h, b * ROWS : (b + 1) * ROWS, :] + bias

        def vis_scores(b, h=h):
            return jnp.where(valid, s_ref[2 * h + 1, b * ROWS : (b + 1) * ROWS, :], MASKED)

        out, log = attend(text_scores, count, p_ref.at[2 * h], tv[0])
        text_out.append(out)
        logs.append(log)
        out, log = attend(vis_scores, count, p_ref.at[2 * h + 1], vv[0])
        vis_out.append(out)
        logs.append(log)
    out_t = jnp.where(lane < HD, text_out[0], text_out[1]).astype(BF16)
    out_v = jnp.where(lane < HD, vis_out[0], vis_out[1]).astype(BF16)
    to[...] = out_t
    vo[...] = out_v
    kept = jnp.zeros((count, PAIR), F32)
    for spot, log in zip((0, 2, 1, 3), logs):
        kept = jnp.where(lane == spot, log, kept)
    lse[0] = kept
    term = mm(jnp.concatenate([out_t, out_v], 1), jnp.concatenate([wo[0], wo[1]], 0))

    accumulate(attn, term)


def forward_rows(first, count, proj, vlen, rel, tables, w_out, deps=(), into=None):
    tqs, tks, tv, vq, vk, vv, hot = proj
    pairs, n, _ = tqs.shape
    d = w_out.shape[2]
    spot = first // count

    def rows_of(x):
        return pl.BlockSpec((1, count, x.shape[2]), lambda p: (p, spot, 0))

    return call(
        partial(forward_body, first=first),
        f"A{spot}",
        (pairs,),
        (vlen, tqs, vq, tks, tv, vk, vv, hot, hot, rel, tables, w_out),
        [
            pl.BlockSpec(memory_space=pltpu.SMEM),
            rows_of(tqs),
            rows_of(vq),
            lead_block(tks),
            lead_block(tv),
            lead_block(vk),
            lead_block(vv),
            pl.BlockSpec((1, count, PAIR), lambda p: (0, spot, 0)),
            whole(hot),
            whole(rel),
            whole(tables),
            pl.BlockSpec((2, PAIR, d), lambda p: (0, p, 0)),
        ],
        [
            sds((count, d)),
            sds((n, pairs * PAIR), BF16),
            sds((n, pairs * PAIR), BF16),
            sds((pairs, n, PAIR)),
        ],
        [
            pl.BlockSpec((count, d), lambda p: (0, 0)),
            pl.BlockSpec((count, PAIR), lambda p: (spot, p)),
            pl.BlockSpec((count, PAIR), lambda p: (spot, p)),
            pl.BlockSpec((1, count, PAIR), lambda p: (p, spot, 0)),
        ],
        [pltpu.VMEM((4, count, n), F32), pltpu.VMEM((4, count, n), BF16)],
        deps=deps,
        aliases=None if into is None else {1: into[1], 2: into[2], 3: into[3]},
    )


def scores_gradient(probs, grad_probs):
    inner = jnp.sum(grad_probs * probs, 1, keepdims=True)
    return (probs * (grad_probs - inner)).astype(BF16)


def box_gradient(hot, spread, out):
    high = spread.astype(BF16)
    rest = (spread - high.astype(F32)).astype(BF16)
    table = (mm_tn(hot, high) + mm_tn(hot, rest))[:NBOX]
    lane = lax.broadcasted_iota(jnp.int32, (NBOX, PAIR), 1)
    for h in range(2):
        mine = table if h == 0 else pltpu.roll(table, NBOX, 1)
        mine = jnp.where(lane < NBOX, mine, 0.0)
        sheared = pltpu.roll(mine, 1, 1, stride=1, stride_axis=0)
        out[0, h : h + 1, :] = jnp.sum(sheared, 0, keepdims=True)


def shear_sum(band):
    width = band.shape[1]
    rows = BLK
    while rows > 8:
        rows //= 2
        band = band[:rows] + pltpu.roll(band[rows:], width - rows, 1)
    row = lax.broadcasted_iota(jnp.int32, band.shape, 0)
    for bit in (4, 2, 1):
        band = jnp.where((row // bit) % 2 == 1, pltpu.roll(band, width - bit, 1), band)
    return jnp.sum(band, 0, keepdims=True)


def visual_back_body(vlen, vq, vk, vv, dvo, lse, hot_q, hot, tables, *refs, last):
    if last:
        before, dxq, dxv, g_box, ds_ref, pb_ref, s_ref, dp_ref = refs
    else:
        dxq, partial_kv, g_box, ds_ref, pb_ref, s_ref, dp_ref = refs
    count = vq.shape[1]
    keys = jnp.concatenate([vk[0], hot[1]], 1)
    valid = lax.broadcasted_iota(jnp.int32, (1, vk.shape[1]), 1) < vlen[0]
    dq = dkt = dvt = spread = None
    for h in range(2):
        mask = head_mask(h, PAIR)
        look = mm_nt(hot_q[0], box_rows(tables, 1, 2 * pl.program_id(0) + h)).astype(BF16)
        mine = vq[0] * mask
        query = jnp.concatenate([mine, look], 1)
        grad = dvo[...] * mask
        s_ref[...] = mm_nt(query, keys)
        dp_ref[...] = mm_nt(grad, vv[0])
        for b in range(count // ROWS):
            part = slice(b * ROWS, (b + 1) * ROWS)
            scores = jnp.where(valid, s_ref[part, :], MASKED)
            probs = jnp.exp(scores - lse[0, part, 2 + h : 3 + h])
            pb_ref[part, :] = probs.astype(BF16)
            ds_ref[part, :] = scores_gradient(probs, dp_ref[part, :])
        ds, pb = ds_ref[...], pb_ref[...]
        terms = (mm(ds, vk[0] * mask), mm_tn(mine, ds), mm_tn(grad, pb), mm(ds, hot[3] * mask))
        if h == 0:
            dq, dkt, dvt, spread = terms
        else:
            dq, dkt, dvt, spread = (a + b for a, b in zip((dq, dkt, dvt, spread), terms))
    box_gradient(hot_q[0], spread, g_box)
    dxq[...] = (dq * SCALE).astype(BF16)
    if last:
        both = jnp.concatenate(
            [(before[0, :PAIR] + dkt).astype(BF16), (before[0, PAIR:] + dvt).astype(BF16)], 0
        ).T
        dxv[...] = both
    else:
        partial_kv[0, :PAIR] = dkt
        partial_kv[0, PAIR:] = dvt


def visual_back(spot, proj, vlen, tables, dvo, lse, before=None, deps=()):
    vq, vk, vv, hot = proj[3:]
    pairs, n, _ = vq.shape
    count = n // 2
    last = before is not None

    def rows_of(x):
        return pl.BlockSpec((1, count, x.shape[2]), lambda p: (p, spot, 0))

    half = pl.BlockSpec((count, PAIR), lambda p: (spot, p))
    args = (vlen, vq, vk, vv, dvo, lse, hot, hot, tables)
    specs = [
        pl.BlockSpec(memory_space=pltpu.SMEM),
        rows_of(vq),
        lead_block(vk),
        lead_block(vv),
        half,
        rows_of(lse),
        pl.BlockSpec((1, count, PAIR), lambda p: (0, spot, 0)),
        whole(hot),
        whole(tables),
    ]
    box = sds((pairs, 8, PAIR))
    kept = sds((pairs, 2 * PAIR, n))
    outs, out_specs = [sds((n, pairs * PAIR), BF16)], [half]
    if last:
        args += (before[1],)
        specs += [lead_block(kept)]
        outs += [sds((n, pairs * 2 * PAIR), BF16), box]
        out_specs += [pair_block(n, 2 * PAIR), lead_block(box)]
    else:
        outs += [kept, box]
        out_specs += [lead_block(kept), lead_block(box)]
    return call(
        partial(visual_back_body, last=last),
        f"V{spot}",
        (pairs,),
        args,
        specs,
        outs,
        out_specs,
        [pltpu.VMEM((count, n), BF16)] * 2 + [pltpu.VMEM((count, n), F32)] * 2,
        deps=deps,
        aliases={0: before[0]} if last else None,
    )


def text_back_body(
    tqs, tks, tv, dto, lse, hot, rel, tables, dxq, dxh, dxs, g_box, g_rel, ds_ref, pb_ref, s_ref, dp_ref, *, pair
):
    n = tqs.shape[1]
    keys = jnp.concatenate([tks[0], hot[0]], 1)
    dq = dkt = dvt = spread = None
    for h in range(2):
        mask, wide_mask = head_mask(h, PAIR), head_mask(h, 2 * PAIR)
        look = mm_nt(hot[0], box_rows(tables, 0, 2 * pair + h)).astype(BF16)
        mine = tqs[0] * wide_mask
        query = jnp.concatenate([mine, look], 1)
        grad = dto[...] * mask
        band, ends = rel_parts(rel, 2 * pair + h)
        near = [None] * 3
        low = high = jnp.zeros((BLK, BLK), F32)
        s_ref[...] = mm_nt(query, keys)
        dp_ref[...] = mm_nt(grad, tv[0])
        for b in range(n // ROWS):
            part = slice(b * ROWS, (b + 1) * ROWS)
            at = b * ROWS
            bias = rel_bias(band, ends, at // BLK, n // BLK, at % BLK)
            probs = jnp.exp(s_ref[part, :] + bias - lse[0, part, h : h + 1])
            pb_ref[part, :] = probs.astype(BF16)
            ds_ref[part, :] = scores_gradient(probs, dp_ref[part, :])
        for b in range(n // BLK):
            ds = ds_ref[b * BLK : (b + 1) * BLK, :].astype(F32)
            for other in range(n // BLK):
                piece = ds[:, other * BLK : (other + 1) * BLK]
                step = other - b
                if step >= 2:
                    high = high + piece
                elif step <= -2:
                    low = low + piece
                else:
                    near[step + 1] = piece if near[step + 1] is None else near[step + 1] + piece
        ds, pb = ds_ref[...], pb_ref[...]
        sums = shear_sum(jnp.concatenate(near + [jnp.zeros((BLK, BLK), F32)], 1))
        far = jnp.concatenate(
            [jnp.sum(low, 0, keepdims=True), jnp.sum(high, 0, keepdims=True)], 1
        )
        g_rel[0, 2 * h : 2 * h + 1, :] = sums
        g_rel[0, 2 * h + 1 : 2 * h + 2, : 2 * BLK] = far
        terms = (mm(ds, tks[0] * wide_mask), mm_tn(mine, ds), mm_tn(grad, pb), mm(ds, hot[2] * mask))
        if h == 0:
            dq, dkt, dvt, spread = terms
        else:
            dq, dkt, dvt, spread = (a + b for a, b in zip((dq, dkt, dvt, spread), terms))
    box_gradient(hot[0], spread, g_box)
    dqs = (dq * SCALE).astype(BF16)
    rest = jnp.concatenate([dkt.astype(BF16), dvt.astype(BF16)], 0).T
    dxs[...] = jnp.concatenate([dqs[:, PAIR:], rest[:, PAIR : 2 * PAIR]], 1)
    dxh[...] = jnp.concatenate([dqs[:, :PAIR], rest[:, :PAIR], rest[:, 2 * PAIR :], dxq[...]], 1)


def text_back(pair, proj, rel, tables, dto, lse, dxq, into=None, deps=()):
    tqs, tks, tv = proj[:3]
    hot = proj[6]
    pairs, n, _ = tqs.shape

    def lead(x):
        return pl.BlockSpec((1,) + x.shape[1:], lambda p: (pair, 0, 0))

    def block(width):
        return pl.BlockSpec((n, width), lambda p: (0, pair))

    outs = [
        sds((n, pairs * 4 * PAIR), BF16),
        sds((n, pairs * 2 * PAIR), BF16),
        sds((pairs, 8, PAIR)),
        sds((pairs, 8, 4 * BLK)),
    ]
    return call(
        partial(text_back_body, pair=pair),
        f"T{pair}",
        (1,),
        (tqs, tks, tv, dto, lse, hot, rel, tables, dxq),
        [lead(tqs), lead(tks), lead(tv), block(PAIR), lead(lse), whole(hot), whole(rel), whole(tables), block(PAIR)],
        outs,
        [block(4 * PAIR), block(2 * PAIR), lead(outs[2]), lead(outs[3])],
        [pltpu.VMEM((n, n), BF16)] * 2 + [pltpu.VMEM((n, n), F32)] * 2,
        deps=deps,
        aliases=None if into is None else {k: into[k] for k in range(4)},
    )


def spatial_part_body(dxs, wt, out):
    accumulate(out, mm_nt(dxs[...], jnp.concatenate([wt[3], wt[4]], 1)))


def spatial_part(dxs, w_text, deps=()):
    n, d = dxs.shape[0], w_text.shape[1]
    return call(
        spatial_part_body,
        "SP",
        (dxs.shape[1] // (2 * PAIR),),
        (dxs, w_text),
        [pair_block(n, 2 * PAIR), pl.BlockSpec((5, d, PAIR), lambda p: (0, 0, p))],
        sds((n, d)),
        pl.BlockSpec((n, d), lambda p: (0, 0)),
        deps=deps,
    )


def visual_part_body(dxv, wv, out):
    accumulate(out, mm_nt(dxv[...], jnp.concatenate([wv[1], wv[2]], 1)))


def visual_part(dxv, w_vis, deps=()):
    n, d = dxv.shape[0], w_vis.shape[1]
    return call(
        visual_part_body,
        "VP",
        (dxv.shape[1] // (2 * PAIR),),
        (dxv, w_vis),
        [pair_block(n, 2 * PAIR), pl.BlockSpec((3, d, PAIR), lambda p: (0, 0, p))],
        sds((n, d)),
        pl.BlockSpec((n, d), lambda p: (0, 0)),
        deps=deps,
    )


def hidden_part_body(dxh, wt, wv, out):
    accumulate(out, mm_nt(dxh[...], jnp.concatenate([wt[0], wt[1], wt[2], wv[0]], 1)))


def hidden_part(dxh, w_text, w_vis, deps=()):
    n, d = dxh.shape[0], w_text.shape[1]
    return call(
        hidden_part_body,
        "HP",
        (dxh.shape[1] // (4 * PAIR),),
        (dxh, w_text, w_vis),
        [
            pair_block(n, 4 * PAIR),
            pl.BlockSpec((5, d, PAIR), lambda p: (0, 0, p)),
            pl.BlockSpec((3, d, PAIR), lambda p: (0, 0, p)),
        ],
        sds((n, d)),
        pl.BlockSpec((n, d), lambda p: (0, 0)),
        deps=deps,
    )


def normalise(values):
    centred = values - jnp.mean(values, 1, keepdims=True)
    rstd = lax.rsqrt(jnp.mean(centred * centred, 1, keepdims=True) + EPSILON)
    return centred * rstd, rstd


def norm_back(grad, unit, rstd, gain):
    scaled = grad * gain
    mean_one = jnp.mean(scaled, 1, keepdims=True)
    mean_two = jnp.mean(scaled * unit, 1, keepdims=True)
    return rstd * (scaled - mean_one - unit * mean_two)


def column_sum(x):
    return jnp.sum(x, 0, keepdims=True)


def up_body(hid, own, got, gain, bias, w_up, b_up, w_down, h1b, z, r1, h1, slope, f):
    @pl.when(pl.program_id(0) == 0)
    def _():
        total = hid[...].astype(F32) + (own[...] + got[...])
        unit, _ = normalise(total)
        normed = unit * gain[0:1, :] + bias[0:1, :]
        r1[...] = total
        h1[...] = normed
        h1b[...] = normed.astype(BF16)

    u = mm(h1b[...], w_up[...]) + b_up[...]
    cdf = 0.5 * (1.0 + lax.erf(u * (0.5**0.5)))
    slope[...] = cdf + u * (jnp.exp(-0.5 * u * u) * 0.3989422804014327)
    active = (u * cdf).astype(BF16)
    z[...] = active
    accumulate(f, mm(active, w_down[...]))


def row_call(
    body, name, spot, grid, args, specs, outs, out_specs, halved, deps, into, far=(), far_in=()
):
    return call(
        body,
        f"{name}{spot}",
        grid,
        args,
        specs,
        outs,
        out_specs,
        deps=deps,
        aliases=None if into is None else {k: into[k] for k in halved},
        far=halved + far,
        far_in=far_in,
    )


def up_rows(spot, hidden, own, got, gain, bias, w_up, b_up, w_down, deps=(), into=None):
    n, d = hidden.shape
    ff = w_up.shape[1]
    count, block = n // 2, ff // FF_STEPS
    half = pl.BlockSpec((count, d), lambda p: (spot, 0))
    own_half = pl.BlockSpec((count, d), lambda p: (0, 0))
    args = (hidden, own, got, gain, bias, w_up, b_up, w_down)
    specs = [half, own_half, own_half, whole(gain), whole(bias), pair_block(d, block)]
    specs += [pair_block(1, block), pl.BlockSpec((block, d), lambda p: (p, 0))]
    outs = [sds((n, d), BF16), sds((n, ff), BF16), sds((count, d)), sds((count, d))]
    outs += [sds((count, ff)), sds((count, d))]
    out_specs = [half, pl.BlockSpec((count, block), lambda p: (spot, p)), own_half, own_half]
    out_specs += [pair_block(count, block), own_half]
    return row_call(
        up_body, "F", spot, (FF_STEPS,), args, specs, outs, out_specs, (0, 1), deps, into, (4,), (0, 5, 7)
    )


def down_body(
    h1, own, got, cot, gain, bias, b_down, w_down, w_up, slope, result, df, du, dr2, pd, sums, sum_up
):
    @pl.when(pl.program_id(0) == 0)
    def _():
        total = h1[...] + ((own[...] + got[...]) + b_down[...])
        unit, rstd = normalise(total)
        result[...] = (unit * gain[1:2, :] + bias[1:2, :]).astype(BF16)
        grad = cot[...].astype(F32)
        back = norm_back(grad, unit, rstd, gain[1:2, :])
        low = back.astype(BF16)
        dr2[...] = back
        df[...] = low
        sums[0:1, :] = column_sum(grad * unit)
        sums[1:2, :] = column_sum(grad)
        sums[2:3, :] = column_sum(low.astype(F32))

    grad_u = (slope[...] * mm_nt(df[...], w_down[...])).astype(BF16)
    du[...] = grad_u
    sum_up[0:1, :] = column_sum(grad_u.astype(F32))
    accumulate(pd, mm_nt(grad_u, w_up[...]))


def down_rows(spot, h1, own, got, cotangent, gain, bias, b_down, w_down, w_up, slope, deps=(), into=None):
    n, d = cotangent.shape
    ff = w_up.shape[1]
    count, block = n // 2, ff // FF_STEPS
    half = pl.BlockSpec((count, d), lambda p: (spot, 0))
    own_half = pl.BlockSpec((count, d), lambda p: (0, 0))
    args = (h1, own, got, cotangent, gain, bias, b_down, w_down, w_up, slope)
    specs = [own_half] * 3 + [half, whole(gain), whole(bias), whole(b_down)]
    specs += [pl.BlockSpec((block, d), lambda p: (p, 0)), pair_block(d, block), pair_block(count, block)]
    outs = [sds((n, d), BF16), sds((n, d), BF16), sds((n, ff), BF16), sds((count, d))]
    outs += [sds((count, d)), sds((8, d)), sds((8, ff))]
    out_specs = [half, half, pl.BlockSpec((count, block), lambda p: (spot, p)), own_half, own_half]
    out_specs += [whole(outs[5]), pair_block(8, block)]
    return row_call(
        down_body,
        "B",
        spot,
        (FF_STEPS,),
        args,
        specs,
        outs,
        out_specs,
        (0, 1, 2),
        deps,
        into,
        far_in=(3, 7, 8, 9),
    )


def first_body(dr2, own, got, r1, gain, w_out, dr1, da, dto, dvo, sums):
    grad = dr2[...] + (own[...] + got[...])
    unit, rstd = normalise(r1[...])
    back = norm_back(grad, unit, rstd, gain[0:1, :])
    low = back.astype(BF16)
    dr1[...] = back
    da[...] = low
    dto[...] = mm_nt(low, w_out[0]).astype(BF16)
    dvo[...] = mm_nt(low, w_out[1]).astype(BF16)
    sums[0:1, :] = column_sum(grad * unit)
    sums[1:2, :] = column_sum(grad)


def first_rows(spot, dr2, own, got, r1, gain, w_out, deps=(), into=None):
    n, d = 2 * own.shape[0], own.shape[1]
    width = w_out.shape[1]
    args = (dr2, own, got, r1, gain, w_out)
    outs = [sds((n, d)), sds((n, d), BF16)]
    outs += [sds((n, width), BF16), sds((n, width), BF16), sds((8, d))]
    out_specs = [pl.BlockSpec((n // 2, x.shape[1]), lambda p: (spot, 0)) for x in outs[:4]] + [whole(outs[4])]
    return row_call(
        first_body,
        "N",
        spot,
        (1,),
        args,
        [whole(x) for x in args],
        outs,
        out_specs,
        (0, 1, 2, 3),
        deps,
        into,
    )


def pack_body(one_a, one_b, two_a, two_b, up_a, up_b, g_rel, g_box_t, g_box_v, g_box_w, out):
    d = out.shape[1]
    one = one_a[...] + one_b[...]
    two = two_a[...] + two_b[...]
    up = up_a[...] + up_b[...]
    out[...] = jnp.zeros(out.shape, F32)
    out[0:1, :] = one[0:1]
    out[1:2, :] = two[0:1]
    out[2:3, :] = one[1:2]
    out[3:4, :] = two[1:2]
    out[4:5, :] = two[2:3]
    out[5:6, :] = up[0:1, :d]
    out[6:7, :] = up[0:1, d:]
    half = NREL // 2
    lane = lax.broadcasted_iota(jnp.int32, (1, 2 * NREL), 1)
    for head in range(2 * g_rel.shape[0]):
        p, h = head // 2, head % 2
        near = g_rel[p, 2 * h : 2 * h + 1, :]
        far = g_rel[p, 2 * h + 1 : 2 * h + 2, :NREL]
        low = jnp.sum(jnp.where((lane > 3 * half) | (lane == 0), near, 0.0), 1, keepdims=True)
        low = low + jnp.sum(far[:, :half], 1, keepdims=True)
        high = jnp.sum(jnp.where((lane >= 2 * half - 1) & (lane < 3 * half), near, 0.0), 1, keepdims=True)
        high = high + jnp.sum(far[:, half:], 1, keepdims=True)
        short = lane[:, :NREL]
        row = jnp.where(short == 0, low, jnp.where(short == NREL - 1, high, near[:, :NREL]))
        spot = 8 + head
        out[spot : spot + 1, :NREL] = row
        out[spot : spot + 1, NREL : NREL + PAIR] = g_box_t[p, h : h + 1, :]
        out[spot : spot + 1, NREL + PAIR : NREL + 2 * PAIR] = (
            g_box_v[p, h : h + 1, :] + g_box_w[p, h : h + 1, :]
        )


def pack_small(d, args, deps=()):
    heads = 2 * args[6].shape[0]
    out = sds((8 + -(-heads // 8) * 8, d))
    return call(
        pack_body, "SK", (1,), args, [whole(x) for x in args], out, whole(out), deps=deps
    )


def unpack_body(own, rel, space, gain, bias, b_up, b_down):
    x = own[...]
    d = x.shape[1]
    gain[...] = x[0:2]
    bias[...] = x[2:4]
    b_down[...] = x[4:5]
    b_up[:, :d] = x[5:6]
    b_up[:, d:] = x[6:7]
    heads = rel.shape[0]
    rel[...] = x[8 : 8 + heads, :NREL]
    space[0] = x[8 : 8 + heads, NREL : NREL + PAIR]
    space[1] = x[8 : 8 + heads, NREL + PAIR : NREL + 2 * PAIR]


def unpack_small(own, heads, ff, deps=()):
    d = own.shape[1]
    outs = [sds((heads, NREL)), sds((2, heads, PAIR)), sds((2, d)), sds((2, d)), sds((1, ff)), sds((1, d))]
    return call(
        unpack_body, "SU", (1,), (own,), [whole(own)], outs, [whole(x) for x in outs], deps=deps
    )


def place_rows(order, left, plain, placed, chunk):
    if chunk is None:
        placed[...] = left[...].T
    else:
        plain[...] = left[...].T
        for r in range(plain.shape[0] // chunk):
            spot = pl.multiple_of(order[r] * chunk, chunk)
            placed[r * chunk : (r + 1) * chunk, :] = plain[pl.ds(spot, chunk), :]


def product_body(order, *refs, sets, chunk):
    count = sum(1 + cols for cols in sets)
    ins, mine = refs[:count], refs[count]
    others, scratch = refs[count + 1 : -2 * len(sets)], refs[-2 * len(sets) :]
    half = mine.shape[0]
    p = pl.program_id(0)
    at = column = 0
    for k, cols in enumerate(sets):
        left, right = ins[at], [c[...] for c in ins[at + 1 : at + 1 + cols]]
        plain, placed = scratch[2 * k : 2 * k + 2]
        at += 1 + cols
        if len(sets) > 1:
            place_rows(order, left, plain, placed, chunk)
        else:

            @pl.when(p == 0)
            def _():
                place_rows(order, left, plain, placed, chunk)

        out = mm(placed[...], right[0] if cols == 1 else jnp.concatenate(right, 1))
        mine[:, column : column + out.shape[1]] = out[:half]
        column += out.shape[1]
        if not others:
            pass
        elif len(sets) > 1:
            others[k][...] = out[half:]
        else:
            for step, other in enumerate(others):

                @pl.when(p == step)
                def _(other=other, out=out):
                    other[...] = out[half:]


def weight_product(name, links, way, sets, steps=1, deps=(), together=False):
    n, d = sets[0][0].shape
    chunk = d // links.n
    order = links.order(way, together)
    args, specs = [order], [pl.BlockSpec(memory_space=pltpu.SMEM)]
    for rows, cols in sets:
        if chunk % 16:
            rows = jnp.take(rows.reshape(n, links.n, chunk), order, axis=1, mode="clip").reshape(n, d)
        args += [rows, *cols]
        specs += [whole(rows)] + [pair_block(n, c.shape[1] // steps) for c in cols]
    widths = [sum(c.shape[1] for c in cols) // steps for _, cols in sets]
    height = d if together else d // 2
    blocks = [] if together else widths * steps
    return call(
        partial(product_body, sets=[len(cols) for _, cols in sets], chunk=None if chunk % 16 else chunk),
        name,
        (steps,),
        tuple(args),
        specs,
        [sds((height, steps * sum(widths)))] + [sds((d // 2, w)) for w in blocks],
        [pair_block(height, sum(widths))] + [pl.BlockSpec((d // 2, w), lambda p: (0, 0)) for w in blocks],
        [pltpu.VMEM((d, n), BF16)] * (2 * len(sets)),
        deps=deps,
    )


def flat(terms):
    return [x for arrays, _ in terms for x in arrays]


def sum_terms(refs, counts):
    total, at = None, 0
    for count in counts:
        pieces = [ref[...] for ref in refs[at : at + count]]
        at += count
        value = pieces[0] if count == 1 else jnp.concatenate(pieces, 1)
        total = value if total is None else total + value
    return total


def add_body(*refs, counts):
    refs[-1][...] = sum_terms(refs[:-1], counts)


def add_chunks(name, terms, rows, first, blocks, deps=()):
    width = sum(x.shape[1] for x in terms[0][0])
    if rows % 8:
        values = [
            jnp.concatenate([x[(at + first) * rows : (at + first + blocks) * rows] for x in arrays], 1)
            for arrays, at in terms
        ]
        return sum(values[1:], values[0])
    step = max(1, blocks // 2)
    args = flat(terms)
    return call(
        partial(add_body, counts=[len(arrays) for arrays, _ in terms]),
        name,
        (blocks // step,),
        tuple(args),
        [
            pl.BlockSpec((step * rows, x.shape[1]), lambda p, at=at: ((at + first) // step + p, 0))
            for arrays, at in terms
            for x in arrays
        ],
        sds((blocks * rows, width)),
        pl.BlockSpec((step * rows, width), lambda p: (p, 0)),
        deps=deps,
    )


def total_body(*refs):
    *first, own, got, out = refs
    total = own[...] + got[...]
    for ref in first:
        total = ref[...] + total
    out[...] = total.astype(out.dtype)


def total_rows(name, spot, own, got, dtype, first=(), deps=(), into=None, parts=2):
    count, d = own.shape
    steps = 4 // parts
    block = pl.BlockSpec((count // steps, d), lambda p: (p, 0))
    placed = pl.BlockSpec((count // steps, d), lambda p: (steps * spot + p, 0))
    return call(
        total_body,
        f"{name}{spot}",
        (steps,),
        (*first, own, got),
        [placed] * len(first) + [block, block],
        sds((parts * count, d), dtype),
        placed,
        deps=deps,
        aliases=None if into is None else {0: into},
    )


def add_small(x, y, deps=()):
    return call(
        partial(add_body, counts=[1, 1]), "SS", (1,), (x, y), [whole(x)] * 2, sds(x.shape), whole(x), deps=deps
    )


class Links:
    def __init__(self, sizes):
        self.n = sizes["dp"]
        bits = [1 << k for k in range(self.n.bit_length() - 1)]
        core, side, *ring = bits
        self.side_first = [core, side, *ring]
        self.ring_first = [core, *ring[:1], side, *ring[1:]]

    def order(self, way, together=False):
        flips = []
        for p in range(self.n):
            flips.append(sum(bit for k, bit in enumerate(way) if p >> (len(way) - 1 - k) & 1))
        me = lax.axis_index("dp")
        return jnp.array(flips, jnp.int32) ^ (me - me % 2 if together else me)

    def cores(self, x):
        groups = [[d, d + 1] for d in range(0, self.n, 2)]
        return lax.all_to_all(x, "dp", 0, 0, axis_index_groups=groups, tiled=True)

    def across(self, x):
        return lax.ppermute(x, "tensor", [(0, 1), (1, 0)])

    def swap(self, x, bit):
        return lax.ppermute(x, "dp", [(d, d ^ bit) for d in range(self.n)])


class Scatter:
    def __init__(self, name, links, way, halves):
        self.name, self.links, self.left = name, links, list(way)
        mine, *others = halves
        self.blocks = links.n // 2
        first = self.left.pop(0)
        if others:
            self.rows = 2 * mine.shape[0] // links.n
            self.terms = [((mine,), 0), (tuple(links.swap(other, first) for other in others), 0)]
        else:
            self.rows = mine.shape[0] // links.n
            both = links.cores(mine)
            self.terms = [((both,), 0), ((both,), self.blocks)]

    def step(self, deps=()):
        if not self.left:
            return deps[0]
        self.blocks //= 2
        name = f"{self.name}{len(self.terms) - 2}"
        out = add_chunks(name, self.terms, self.rows, self.blocks, self.blocks, deps)
        self.terms.append(((self.links.swap(out, self.left.pop(0)),), 0))
        return out

    def rest(self, deps=()):
        while self.left:
            deps = (self.step(deps),)
        return deps

    def total(self, deps=()):
        deps = self.rest(deps)
        return add_chunks(f"{self.name}T", self.terms, self.rows, 0, 1, deps)


def spread_body(*refs, counts, places, ready):
    groups = [sum(c) for c in counts]
    ins, out_refs = refs[: sum(groups)], refs[sum(groups) + len(ready) :]
    for ref, (out, m) in zip(refs[sum(groups) :], ready):
        out_refs[out][m : m + ref.shape[0]] = ref[...]
    at = 0
    for count, place in zip(counts, places):
        total = sum_terms(ins[at : at + sum(count)], count)
        at += sum(count)
        for k, (out, m, p) in enumerate(place):
            out_refs[out][m, :, p * PAIR : (p + 1) * PAIR] = total[:, k * PAIR : (k + 1) * PAIR]


def spread(name, scatters, places, outs, deps=(), ready=()):
    rows = scatters[0].rows
    for s in scatters:
        deps = s.rest(deps)
    if rows % 8:
        parts = {}
        for s, place in zip(scatters, places):
            total = s.total(deps)
            for k, key in enumerate(place):
                parts[key] = total[:, k * PAIR : (k + 1) * PAIR]
        for x, out, first in ready:
            for m in range(x.shape[0]):
                for p in range(x.shape[2] // PAIR):
                    parts[out, first + m, p] = x[m, :, p * PAIR : (p + 1) * PAIR]
        return [
            jnp.stack(
                [
                    jnp.concatenate([parts[o, m, p] for p in range(x.shape[2] // PAIR)], 1)
                    for m in range(x.shape[0])
                ]
            )
            for o, x in enumerate(outs)
        ]
    args = [x for s in scatters for x in flat(s.terms)]
    return call(
        partial(
            spread_body,
            counts=[[len(t) for t, _ in s.terms] for s in scatters],
            places=places,
            ready=[(out, first) for _, out, first in ready],
        ),
        name,
        (1,),
        (*args, *(x for x, _, _ in ready)),
        [
            pl.BlockSpec((rows, x.shape[1]), lambda p, at=at: (at, 0))
            for s in scatters
            for arrays, at in s.terms
            for x in arrays
        ]
        + [whole(x) for x, _, _ in ready],
        outs,
        [whole(x) for x in outs],
        deps=deps,
        far_in=range(len(args) + len(ready)),
    )


def on_device(
    links,
    hidden,
    spatial,
    visual,
    vis_len,
    text_box,
    vis_box,
    text_weight_matrix,
    w_vis,
    w_out,
    rel_table,
    space_tables,
    norm_gain,
    norm_bias,
    w_up,
    b_up,
    w_down,
    b_down,
    cotangent,
):
    Plan.begin()
    n, d = hidden.shape
    width = w_vis.shape[2]
    pairs = width // PAIR
    ff = w_up.shape[1]
    heads = rel_table.shape[0]
    text_row, vis_row = text_box.reshape(1, n), vis_box.reshape(1, -1)
    b_up_row, b_down_row = b_up.reshape(1, ff), b_down.reshape(1, d)

    proj = projections(hidden, spatial, visual, text_weight_matrix, w_vis, text_row, vis_row)
    count = n // 2
    common = (proj, vis_len, rel_table, space_tables, w_out)
    front_a = forward_rows(0, count, *common)
    got_a = links.across(front_a[0])
    front_b = forward_rows(count, count, *common, deps=(front_a[0],), into=front_a)
    got_b = links.across(front_b[0])
    merged_t, merged_v, lse = front_b[1:]

    feed = (norm_gain, norm_bias, w_up, b_up_row, w_down)
    up_a = up_rows(0, hidden, front_a[0], got_a, *feed, deps=(front_b[0],))
    got_a = links.across(up_a[5])
    up_b = up_rows(1, hidden, front_b[0], got_b, *feed, deps=(up_a[5],), into=up_a)
    got_b = links.across(up_b[5])
    h1_low, active = up_b[:2]

    feed = (cotangent, norm_gain, norm_bias, b_down_row, w_down, w_up)
    down_a = down_rows(0, up_a[3], up_a[5], got_a, *feed, up_a[4], deps=(up_b[5],))
    got_a = links.across(down_a[4])
    down_b = down_rows(1, up_b[3], up_b[5], got_b, *feed, up_b[4], deps=(down_a[4],), into=down_a)
    got_b = links.across(down_b[4])
    result, df, du = down_b[:3]

    way_a, way_b = links.side_first, links.ring_first
    half_down = weight_product("pD", links, way_a, [(df, (active,))], 2, (down_b[4],))
    sc_down = Scatter("D", links, way_a, half_down)
    half_up = weight_product("pU", links, way_b, [(h1_low, (du,))], 2, half_down[:1])
    sc_up = Scatter("U", links, way_b, half_up)
    first_a = first_rows(
        0, down_a[3], down_a[4], got_a, up_a[2], norm_gain, w_out, deps=half_up[:1]
    )
    last = sc_down.step((first_a[4],))
    last = sc_up.step((last,))
    vis_a = visual_back(0, proj, vis_len, space_tables, first_a[3], lse, deps=(last,))
    first_b = first_rows(
        1, down_b[3], down_b[4], got_b, up_b[2], norm_gain, w_out, deps=vis_a[1:2], into=first_a
    )
    dr1, da, dto, dvo = first_b[:4]
    dxq, dxv, g_box_vis = visual_back(
        1, proj, vis_len, space_tables, dvo, lse, before=vis_a, deps=(first_b[4],)
    )
    half_mixed = weight_product(
        "pM",
        links,
        way_a,
        [(da, (merged_t, merged_v)), (visual, (dxv,))],
        1,
        (g_box_vis,),
    )
    sc_mixed = Scatter("M", links, way_a, half_mixed)
    part_vis = visual_part(dxv, w_vis, half_mixed[:1])
    got_vis = links.across(part_vis)
    last = sc_down.step((part_vis,))
    last = sc_up.step((last,))
    text = text_back(0, proj, rel_table, space_tables, dto, lse, dxq, None, (last,))
    last = sc_mixed.step((text[2],))
    text = text_back(1, proj, rel_table, space_tables, dto, lse, dxq, text, (last,))
    dxh, dxs, g_box_text, g_rel = text_back(
        2, proj, rel_table, space_tables, dto, lse, dxq, text, text[2:3]
    )
    last = small = pack_small(
        d,
        (first_a[4], first_b[4], down_a[5], down_b[5], down_a[6], down_b[6])
        + (g_rel, g_box_text, vis_a[2], g_box_vis),
    )
    bits = list(links.side_first)

    def small_step(x, deps):
        return add_small(x, links.swap(x, bits.pop(0)), deps)

    part_spa = spatial_part(dxs, text_weight_matrix, (last,))
    got_spa = links.across(part_spa)
    last = sc_up.step((part_spa,))
    last = sc_down.step((last,))
    half_hid = weight_product(
        "pH", links, way_a, [(hidden, (dxh,))], 2, (last,), together=True
    )
    sc_hid = Scatter("H", links, way_a, half_hid)
    last = sc_hid.step(half_hid[:1])
    last = grad_visual = total_rows("VT", 0, part_vis, got_vis, F32, deps=(last,), parts=1)
    last = sc_mixed.step((last,))
    last = g_w_up = sc_up.total((last,))
    half_spa = weight_product(
        "pS", links, way_b, [(spatial, (dxs,))], 1, (last,), together=True
    )
    sc_spa = Scatter("S", links, way_b, half_spa)
    last = sc_spa.step(half_spa[:1])
    last = g_w_down = sc_down.total((last,))
    part_hid = hidden_part(dxh, text_weight_matrix, w_vis, (last,))
    got_hid = links.across(part_hid)
    last = sc_mixed.step((part_hid,))
    last = sc_hid.step((last,))
    last = sc_spa.step((last,))
    last = grad_spatial = total_rows("ST", 0, part_spa, got_spa, F32, deps=(last,), parts=1)
    last = small = small_step(small, (last,))
    last = small = small_step(small, (last,))
    rows = d // links.n
    three = range(pairs)
    g_w_out, g_vis = spread(
        "MT",
        [sc_mixed],
        [[(0, m, p) for m in range(2) for p in three] + [(1, m, p) for p in three for m in range(2)]],
        [sds((2, rows, width))] * 2,
        (last,),
    )
    last = sc_spa.step((g_vis,))
    last = sc_hid.step((last,))
    last = small = small_step(small, (last,))
    last = grad_hidden = total_rows("HT", 0, part_hid, got_hid, BF16, (dr1,), deps=(last,), parts=1)
    while bits:
        last = small = small_step(small, (last,))
    last, *_ = g_rel_table, g_space, g_gain, g_bias, g_b_up, g_b_down = unpack_small(
        small, rel_table.shape[0], ff, (last,)
    )
    g_w_text, g_w_vis = spread(
        "AT",
        [sc_hid, sc_spa],
        [
            [((0, m, p) if m < 3 else (1, 0, p)) for p in three for m in range(4)],
            [(0, 3 + m, p) for p in three for m in range(2)],
        ],
        [sds((5, rows, width)), sds((3, rows, width))],
        (last,),
        [(g_vis, 1, 1)],
    )
    return (
        result,
        grad_hidden,
        grad_spatial,
        grad_visual,
        g_w_text,
        g_w_vis,
        g_w_out.transpose(0, 2, 1),
        g_rel_table,
        g_space,
        g_gain,
        g_bias,
        g_w_up,
        g_b_up.reshape(ff),
        g_w_down.T,
        g_b_down.reshape(d),
    )


def solution(mesh):
    return jax.shard_map(
        partial(on_device, Links(dict(mesh.shape))),
        mesh=mesh,
        in_specs=(
            P("dp", None),
            P("dp", None),
            P("dp", None),
            P("dp"),
            P("dp"),
            P("dp"),
            P(None, None, "tensor"),
            P(None, None, "tensor"),
            P(None, "tensor", None),
            P("tensor", None),
            P(None, "tensor", None),
            P(),
            P(),
            P(None, "tensor"),
            P("tensor"),
            P("tensor", None),
            P(),
            P("dp", None),
        ),
        out_specs=(
            P("dp", None),
            P("dp", None),
            P("dp", None),
            P("dp", None),
            P(None, "dp", "tensor"),
            P(None, "dp", "tensor"),
            P(None, "tensor", "dp"),
            P("tensor", None),
            P(None, "tensor", None),
            P(),
            P(),
            P("dp", "tensor"),
            P("tensor"),
            P("tensor", "dp"),
            P(),
        ),
        check_vma=False,
    )
```
